32 devices in a mesh: group: 2 (over y), seq: 8 (over z, x), tensor: 2 (over core).
Axes of the slice: x: 2, y: 2, z: 4, core: 2. Of those that a mesh axis runs over, the one named last changes fastest.
Arguments:
- streams: bfloat16 [3, 128, 16, 2048], P(None, 'seq', 'group', 'tensor'), parts along dimension 2, may hold values from -6 to 6
- short_taps: float32 [3, 3, 2048], P(None, None, 'tensor'), may hold values from -3 to 3
- long_filters: bfloat16 [2, 128, 8, 2048], P(None, 'seq', None, 'tensor'), may hold values from -0.1875 to 0.1875
- out_grad: bfloat16 [128, 16, 2048], P('seq', 'group', 'tensor'), parts along dimension 1, may hold values from -6 to 6
Outputs:
- layer_out: bfloat16 [128, 16, 2048], P('seq', 'group', 'tensor'), parts along dimension 1
- stream_grads: bfloat16 [3, 128, 16, 2048], P(None, 'seq', 'group', 'tensor'), parts along dimension 2
- tap_grads: float32 [6, 3, 2048], P('group', None, 'tensor'), parts along dimension 0
The draws below stay inside these ranges and needn't reach their ends.
There are 2 independent parts, one for each index of `group`. The reference program is written for one: setup_inputs(seed, part) draws one part's arguments, and reference() takes and returns one part's arrays. A program takes and returns all parts, laid end to end along the dimension named above; an argument that names none is the same for every part. Nothing has to cross between parts.
All inputs are finite; a program needn't handle non-finite values.
Results may differ from the reference program's by a relative error of at most 0.0064.
Values may be sent and summed in bfloat16 or wider, within the bound.
A program may use at most 64 MiB of HBM per device.

```python
import math
import jax
import jax.numpy as jnp
from jax import lax

DW = 2048
ROWS = 128
STREAMS = 3
TAPS = 3
BLOCKS = 8
SEQ = 1024


def block_scale(stream_key, dims, shards, low, high):
    level = 1.0
    for dim, parts in shards:
        steps = jax.random.uniform(jax.random.fold_in(jax.random.fold_in(stream_key, 6), dim), (parts,), jnp.float32, low / len(shards), high / len(shards))
        level = level * jnp.repeat(jnp.exp(steps), dims[dim] // parts).reshape((-1,) + (1,) * (len(dims) - 1 - dim))
    return level


def normal_values(own_key, extent, scale, reach, shards=(), held_as=jnp.bfloat16):
    values = jax.random.normal(own_key, extent, jnp.float32) * scale
    if len(shards) > 0:
        values = block_scale(own_key, extent, shards, -0.22, 0.18) * values
    return jnp.clip(values, min=-reach, max=reach).astype(held_as)


def setup_inputs(seed: int = 0, part: int = 0) -> dict:
    keys = jax.random.split(jax.random.key(seed), 5)
    own_keys = jax.random.split(jax.random.fold_in(keys[4], part), 5)
    return {
        "streams": normal_values(own_keys[0], (STREAMS, ROWS, BLOCKS, DW), 1.0, 6.0, ((1, 8), (3, 2))),
        "short_taps": normal_values(keys[1], (STREAMS, TAPS, DW), 0.6, 3.0, ((2, 2),), jnp.float32),
        "long_filters": normal_values(keys[2], (2, ROWS, BLOCKS, DW), (SEQ ** -0.5), 0.1875, ((1, 8), (3, 2))),
        "out_grad": normal_values(own_keys[3], (ROWS, BLOCKS, DW), 1.0, 6.0, ((0, 8), (2, 2))),
    }


def to_time(field):
    moved = jnp.swapaxes(field, -3, -2)
    return moved.reshape(moved.shape[:-3] + (-1, moved.shape[-1]))

def to_layout(field):
    blocked = field.reshape(field.shape[:-2] + (BLOCKS, ROWS, field.shape[-1]))
    return jnp.swapaxes(blocked, -3, -2)

def earlier(field, steps):
    padding = jnp.zeros_like(field[..., :steps, :])
    return jnp.concatenate([padding, field[..., :-steps, :]], axis=-2)

def later(field, steps):
    padding = jnp.zeros_like(field[..., :steps, :])
    return jnp.concatenate([field[..., steps:, :], padding], axis=-2)

def causal(kernel, signal):
    length = signal.shape[0]
    padded = 2 * length
    spectrum = jnp.fft.rfft(kernel, n=padded, axis=0) * jnp.fft.rfft(signal, n=padded, axis=0)
    return jnp.fft.irfft(spectrum, n=padded, axis=0)[:length]

def backwards(kernel, signal):
    return jnp.flip(causal(kernel, jnp.flip(signal, 0)), 0)

def reference(streams, short_taps, long_filters, out_grad):
    inputs = to_time(streams).astype(jnp.float32)
    prev_one = earlier(inputs, 1)
    prev_two = earlier(inputs, 2)
    tap_zero = short_taps[:, 0][:, None, :]
    tap_one = short_taps[:, 1][:, None, :]
    tap_two = short_taps[:, 2][:, None, :]
    filtered = (tap_zero * inputs + tap_one * prev_one + tap_two * prev_two).astype(jnp.bfloat16)
    filtered = filtered.astype(jnp.float32)
    value_stream = filtered[0]
    gate_one = filtered[1]
    gate_two = filtered[2]
    filters = to_time(long_filters).astype(jnp.float32)
    first_conv = causal(filters[0], value_stream)
    gated = gate_one * first_conv
    second_conv = causal(filters[1], gated)
    layer_out = (gate_two * second_conv).astype(jnp.bfloat16)
    cotangent = to_time(out_grad).astype(jnp.float32)
    back_two = cotangent * gate_two
    grad_two = cotangent * second_conv
    grad_gated = backwards(filters[1], back_two)
    grad_one = grad_gated * first_conv
    back_one = grad_gated * gate_one
    grad_value = backwards(filters[0], back_one)
    stream_cot = jnp.stack([grad_value, grad_one, grad_two]).astype(jnp.bfloat16).astype(jnp.float32)
    stream_grads = (tap_zero * stream_cot + tap_one * later(stream_cot, 1) + tap_two * later(stream_cot, 2)).astype(jnp.bfloat16)
    tap_terms = jnp.stack([lax.optimization_barrier(jnp.sum(stream_cot * inputs, axis=1)), lax.optimization_barrier(jnp.sum(stream_cot * prev_one, axis=1)), lax.optimization_barrier(jnp.sum(stream_cot * prev_two, axis=1))], axis=1)
    tap_grads = tap_terms * (1.0 / math.sqrt(SEQ))
    return (to_layout(layer_out), to_layout(stream_grads), tap_grads)
```

```python
import functools
import math

import jax
import jax.numpy as jnp
import ml_dtypes
import numpy as np
from jax import lax
from jax.experimental import pallas as pl
from jax.experimental.pallas import tpu as pltpu
from jax.sharding import PartitionSpec as P

HIGHEST_PRECISION = lax.Precision.HIGHEST
MESH = pl.DeviceIdType.MESH
LANES = 128
TILE = 256
F32 = jnp.float32
BF16 = jnp.bfloat16


def shifted(value, axis, by):
    count = lax.axis_size(axis)
    return lax.ppermute(value, axis, [(i, (i + by) % count) for i in range(count)])


def complex_product(left_real, left_imag, right_real, right_imag):
    return (
        left_real * right_real - left_imag * right_imag,
        left_real * right_imag + left_imag * right_real,
    )


def conj_product(left_real, left_imag, right_real, right_imag):
    return (
        left_real * right_real + left_imag * right_imag,
        left_real * right_imag - left_imag * right_real,
    )


def local(streams, short_taps, long_filters, out_grad):
    seq_count = lax.axis_size("seq")
    seq_place = lax.axis_index("seq")
    local_rows = streams.shape[1]
    channels = streams.shape[3]
    block_rows = local_rows * seq_count
    full_length = 2 * block_rows * seq_count
    angle_unit = math.pi / full_length
    block_pos = jnp.arange(seq_count, dtype=jnp.int32)
    odd_slots = 2 * block_pos + 1
    local_index = seq_place * local_rows + jnp.arange(local_rows, dtype=jnp.int32)
    row_pos = jnp.arange(block_rows, dtype=jnp.int32)
    start_pos = block_pos[None, :, None] * block_rows + local_index[:, None, None]
    fwd_angle = (start_pos * odd_slots[None, None, :] % (2 * full_length)).astype(
        jnp.float32
    ) * angle_unit
    fwd_table = jnp.stack([jnp.cos(fwd_angle), -jnp.sin(fwd_angle)], axis=-1)
    inner_angle = (row_pos[:, None] * row_pos[None, :] % block_rows).astype(jnp.float32) * (
        2.0 * math.pi / block_rows
    )
    inner_cos = jnp.cos(inner_angle)
    inner_sin = jnp.sin(inner_angle)
    inner_table = jnp.stack(
        [jnp.stack([inner_cos, -inner_sin], axis=-1), jnp.stack([inner_sin, inner_cos], axis=-1)],
        axis=0,
    )
    back_num = (
        row_pos[None, :]
        * (4 * seq_count * row_pos[:, None] + 2 * seq_place + 1)
        % (2 * full_length)
    )
    back_angle = back_num.astype(jnp.float32) * angle_unit
    back_cos = jnp.cos(back_angle)
    back_sin = jnp.sin(back_angle)
    back_table = jnp.stack(
        [jnp.stack([back_cos, back_sin], axis=-1), jnp.stack([-back_sin, back_cos], axis=-1)],
        axis=0,
    )
    outer_angle = (block_pos[:, None] * odd_slots[None, :] % (4 * seq_count)).astype(
        jnp.float32
    ) * (math.pi / (2 * seq_count))
    outer_table = jnp.stack([jnp.cos(outer_angle).T, -jnp.sin(outer_angle).T], axis=0)

    def previous_rows(block):
        edge = shifted(block[:, -1:], "seq", 1)
        rolled = jnp.concatenate([jnp.zeros_like(edge[:, :, :1]), edge[:, :, :-1]], axis=2)
        edge = jnp.where(seq_place == 0, rolled, edge)
        return jnp.concatenate([edge, block[:, :-1]], axis=1)

    def next_rows(block):
        edge = shifted(block[:, :1], "seq", -1)
        rolled = jnp.concatenate([edge[:, :, 1:], jnp.zeros_like(edge[:, :, :1])], axis=2)
        edge = jnp.where(seq_place == seq_count - 1, rolled, edge)
        return jnp.concatenate([block[:, 1:], edge], axis=1)

    def spectra(signals):
        count = signals.shape[0]
        twisted = jnp.einsum("simc,imjr->srijc", signals, fwd_table, precision=HIGHEST_PRECISION)
        slotted = lax.all_to_all(twisted, "seq", split_axis=3, concat_axis=2, tiled=True)
        slotted = slotted.reshape(count, 2, block_rows, channels)
        spec = jnp.einsum("sric,rikq->sqkc", slotted, inner_table, precision=HIGHEST_PRECISION)
        return (spec[:, 0], spec[:, 1])

    def signals_back(real_spec, imag_spec):
        count = real_spec.shape[0]
        stacked = jnp.stack([real_spec, imag_spec], axis=1)
        turned = jnp.einsum("srkc,rkiq->sqic", stacked, back_table, precision=HIGHEST_PRECISION)
        turned = turned.reshape(count, 2, block_rows, 1, channels)
        parts = lax.all_to_all(turned, "seq", split_axis=2, concat_axis=3, tiled=True)
        rows_out = jnp.einsum("srijc,rjm->simc", parts, outer_table, precision=HIGHEST_PRECISION)
        return rows_out * (2.0 / full_length)

    def tap_weight(index):
        return short_taps[:, index][:, None, None, :]

    prev_one = previous_rows(streams)
    prev_two = previous_rows(prev_one)
    filtered = (
        tap_weight(0) * streams + tap_weight(1) * prev_one + tap_weight(2) * prev_two
    ).astype(jnp.bfloat16)
    value_stream = filtered[0].astype(jnp.float32)
    gate_one = filtered[1].astype(jnp.float32)
    gate_two = filtered[2].astype(jnp.float32)
    filters = long_filters.astype(jnp.float32)
    real_first, imag_first = spectra(jnp.stack([value_stream, filters[0]]))
    product_one = complex_product(real_first[0], imag_first[0], real_first[1], imag_first[1])
    first_conv = signals_back(product_one[0][None], product_one[1][None])[0]
    gated_first = gate_one * first_conv
    real_second, imag_second = spectra(jnp.stack([gated_first, filters[1]]))
    product_two = complex_product(real_second[0], imag_second[0], real_second[1], imag_second[1])
    second_conv = signals_back(product_two[0][None], product_two[1][None])[0]
    layer_out = (gate_two * second_conv).astype(jnp.bfloat16)
    cotangent = out_grad.astype(jnp.float32)
    back_two = cotangent * gate_two
    grad_two = cotangent * second_conv
    real_third, imag_third = spectra(back_two[None])
    filter_two_real, filter_two_imag = (real_second[1], imag_second[1])
    correlated_two = conj_product(filter_two_real, filter_two_imag, real_third[0], imag_third[0])
    grad_gated = signals_back(correlated_two[0][None], correlated_two[1][None])[0]
    grad_one = grad_gated * first_conv
    back_one = grad_gated * gate_one
    real_fourth, imag_fourth = spectra(back_one[None])
    filter_one_real, filter_one_imag = (real_first[1], imag_first[1])
    correlated_one = conj_product(filter_one_real, filter_one_imag, real_fourth[0], imag_fourth[0])
    grad_value = signals_back(correlated_one[0][None], correlated_one[1][None])[0]
    stream_cot = jnp.stack([grad_value, grad_one, grad_two]).astype(jnp.bfloat16)
    next_one = next_rows(stream_cot)
    next_two = next_rows(next_one)
    stream_grads = (
        tap_weight(0) * stream_cot + tap_weight(1) * next_one + tap_weight(2) * next_two
    ).astype(jnp.bfloat16)
    cot_float = stream_cot.astype(jnp.float32)
    tap_terms = jnp.stack(
        [
            jnp.sum(cot_float * streams, axis=(1, 2)),
            jnp.sum(cot_float * prev_one, axis=(1, 2)),
            jnp.sum(cot_float * prev_two, axis=(1, 2)),
        ],
        axis=1,
    )
    tap_total = lax.psum(tap_terms, "seq")
    return (layer_out, stream_grads, tap_total * (1.0 / math.sqrt(block_rows * seq_count)))


def dft_tables(blocks, rows):
    length = blocks * rows
    place = np.arange(length)
    time = (place % blocks) * rows + place // blocks
    half = TILE // 2
    freq = np.arange(length).reshape(-1, half)
    angle = ((2 * freq[:, :, None] + 1) * time[None, None, :] % (4 * length)) * (math.pi / (2 * length))
    table = np.concatenate([np.cos(angle), -np.sin(angle)], axis=1).reshape(2 * length, length)
    return (
        table.astype(ml_dtypes.bfloat16),
        np.ascontiguousarray(table.T / length).astype(ml_dtypes.bfloat16),
    )


FILTER0, FILTER1, VALUE, GATE_TWO, OUT_GRAD, GATE_ONE, SG_ONE, LAYER, SG_TWO, SG_VALUE, TAPS_OUT = range(11)


def kernel(
    seq, blocks, streams, taps, filters, out_grad, fwd_hbm, inv_hbm,
    layer_out, stream_grads, tap_out,
    fwd, inv, xf, sb, og, s32, cot, gates, sig, spec_f, prod, conv, conv2, staged, tap_send,
    send_sem, recv_sem, table_sem,
):
    me = lax.axis_index("seq")
    part = streams.shape[1]
    length = part * seq
    half = TILE // 2
    order = sorted(range(1, seq), key=lambda k: abs(k - seq / 2))

    def peer(k):
        return lax.rem(me + k, seq)

    def lanes(d):
        return pl.ds(pl.multiple_of(d * LANES, LANES), LANES)

    def rows(d):
        return pl.ds(pl.multiple_of(d * part, part), part)

    def remote(slot, k, src, dst):
        return pltpu.make_async_remote_copy(
            src_ref=src, dst_ref=dst, send_sem=send_sem.at[slot, k], recv_sem=recv_sem.at[slot, k],
            device_id={"seq": peer(k)}, device_id_type=MESH,
        )

    def exchange(slot, src_of, dst):
        own = pltpu.make_async_copy(src_of(me), dst, recv_sem.at[slot, 0])
        copies = [remote(slot, k, src_of(peer(k)), dst) for k in order]
        for copy in copies:
            copy.start()
        own.start()
        return own, copies

    def arrive(exchanged):
        own, copies = exchanged
        own.wait()
        for copy in copies:
            copy.wait_recv()

    barrier = pltpu.get_barrier_semaphore()
    for k in range(1, seq):
        pl.semaphore_signal(barrier, inc=1, device_id={"seq": peer(k)}, device_id_type=MESH)
    fwd_copy = pltpu.make_async_copy(fwd_hbm, fwd, table_sem.at[0])
    inv_copy = pltpu.make_async_copy(inv_hbm, inv, table_sem.at[1])
    fwd_copy.start()
    inv_copy.start()
    pl.semaphore_wait(barrier, seq - 1)

    mine = rows(me)
    in_f0 = exchange(FILTER0, lambda d: filters.at[0, :, lanes(d)], xf.at[mine, pl.ds(0, LANES)])
    in_f1 = exchange(FILTER1, lambda d: filters.at[1, :, lanes(d)], xf.at[mine, pl.ds(LANES, LANES)])
    in_v = exchange(VALUE, lambda d: streams.at[0, :, lanes(d)], sb.at[0, mine])
    in_g2 = exchange(GATE_TWO, lambda d: streams.at[2, :, lanes(d)], sb.at[2, mine])
    in_og = exchange(OUT_GRAD, lambda d: out_grad.at[:, lanes(d)], og.at[mine])
    in_g1 = exchange(GATE_ONE, lambda d: streams.at[1, :, lanes(d)], sb.at[1, mine])
    sent = [in_f0, in_f1, in_v, in_g2, in_og, in_g1]

    pad = 2 * blocks
    sub = lax.broadcasted_iota(jnp.int32, (blocks, LANES), 0)

    def tap(s, j):
        return taps[pl.ds(3 * s + j, 1), lanes(me)]

    def chunk(c):
        return pl.ds(pl.multiple_of(c * part, part), part)

    def offset(c, by):
        return pl.ds(pl.multiple_of(c * part + by, blocks), part)

    def widen(s):
        def body(c, carry):
            s32[s, offset(c, pad), :] = sb[s, chunk(c), :].astype(F32)
            return carry

        lax.fori_loop(0, seq, body, 0)
        for step in range(2):
            edge = s32[s, pl.ds(length + step * blocks, blocks), :]
            s32[s, pl.ds(step * blocks, blocks), :] = jnp.where(sub == 0, 0.0, pltpu.roll(edge, 1, 0))

    def filtered(s, c):
        total = tap(s, 0) * s32[s, offset(c, pad), :]
        total = total + tap(s, 1) * s32[s, offset(c, blocks), :]
        total = total + tap(s, 2) * s32[s, offset(c, 0), :]
        return total.astype(BF16)

    def cots(s, c):
        base = [cot[s, offset(c, j * blocks), :] for j in range(3)]
        total = tap(s, 0) * base[0] + tap(s, 1) * base[1] + tap(s, 2) * base[2]
        return total.astype(BF16)

    def close(s):
        for step in range(2):
            edge = cot[s, pl.ds(step * blocks, blocks), :]
            cot[s, pl.ds(length + step * blocks, blocks), :] = jnp.where(
                sub == blocks - 1, 0.0, pltpu.roll(edge, blocks - 1, 0)
            )

    def grads_of(s, slot):
        def body(c, sums):
            staged[slot, chunk(c), :] = cots(s, c)
            now = cot[s, offset(c, 0), :]
            return tuple(
                sums[j]
                + jnp.sum(
                    (now * s32[s, offset(c, pad - j * blocks), :]).reshape(-1, 8, LANES), axis=0
                )
                for j in range(3)
            )

        sums = lax.fori_loop(0, seq, body, tuple(jnp.zeros((8, LANES), F32) for _ in range(3)))
        for j in range(3):
            tap_send[pl.ds(3 * s + j, 1), :] = jnp.sum(sums[j], axis=0, keepdims=True) * (
                1.0 / math.sqrt(length)
            )

    def tile(m):
        return pl.ds(pl.multiple_of(m * TILE, TILE), TILE)

    def forward(m, signals):
        out = jnp.dot(fwd[tile(m), :], signals[...], preferred_element_type=F32)
        return out[:half], out[half:]

    def put(m, col, real, imag):
        prod[pl.ds(pl.multiple_of(m * TILE, TILE), half), col * LANES:(col + 1) * LANES] = real.astype(BF16)
        prod[pl.ds(pl.multiple_of(m * TILE + half, half), half), col * LANES:(col + 1) * LANES] = imag.astype(BF16)

    def spectra_of(m, col):
        cols = slice(col * LANES, (col + 1) * LANES)
        return (
            spec_f[pl.ds(pl.multiple_of(m * TILE, TILE), half), cols],
            spec_f[pl.ds(pl.multiple_of(m * TILE + half, half), half), cols],
        )

    def inverse(into):
        def body(m, carry):
            into[tile(m), :] = jnp.dot(inv[tile(m), :], prod[...], preferred_element_type=F32)
            return carry

        lax.fori_loop(0, length // TILE, body, 0)

    fwd_copy.wait()
    arrive(in_f0)
    arrive(in_f1)

    def filter_body(m, carry):
        spec_f[tile(m), :] = jnp.dot(fwd[tile(m), :], xf[...], preferred_element_type=F32)
        return carry

    lax.fori_loop(0, 2 * length // TILE, filter_body, 0)

    arrive(in_v)
    widen(0)

    def value_body(c, carry):
        sig[chunk(c), 0:LANES] = filtered(0, c)
        return carry

    lax.fori_loop(0, seq, value_body, 0)
    arrive(in_g2)
    widen(2)

    arrive(in_og)

    def back_body(c, carry):
        gate = filtered(2, c)
        gates[1, chunk(c), :] = gate.astype(F32)
        sig[chunk(c), LANES:] = (og[chunk(c), :].astype(F32) * gate.astype(F32)).astype(BF16)
        return carry

    lax.fori_loop(0, seq, back_body, 0)

    def first_body(m, carry):
        real, imag = forward(m, sig)
        f0r, f0i = spectra_of(m, 0)
        f1r, f1i = spectra_of(m, 1)
        vr, vi, br, bi = real[:, :LANES], imag[:, :LANES], real[:, LANES:], imag[:, LANES:]
        put(m, 0, *complex_product(vr, vi, f0r, f0i))
        put(m, 1, *conj_product(f1r, f1i, br, bi))
        return carry

    lax.fori_loop(0, 2 * length // TILE, first_body, 0)
    inv_copy.wait()
    inverse(conv)

    def one_body(c, carry):
        both = conv[chunk(c), :]
        cot[1, offset(c, 0), :] = (both[:, LANES:] * both[:, :LANES]).astype(BF16).astype(F32)
        return carry

    lax.fori_loop(0, seq, one_body, 0)
    close(1)
    arrive(in_g1)
    widen(1)
    grads_of(1, 2)
    out_one = exchange(SG_ONE, lambda d: staged.at[2, rows(d)], stream_grads.at[1, :, lanes(me)])

    def gated_body(c, carry):
        gate = filtered(1, c).astype(F32)
        both = conv[chunk(c), :]
        sig[chunk(c), 0:LANES] = (gate * both[:, :LANES]).astype(BF16)
        sig[chunk(c), LANES:] = (gate * both[:, LANES:]).astype(BF16)
        return carry

    lax.fori_loop(0, seq, gated_body, 0)

    def second_body(m, carry):
        real, imag = forward(m, sig)
        f0r, f0i = spectra_of(m, 0)
        f1r, f1i = spectra_of(m, 1)
        gr, gi, br, bi = real[:, :LANES], imag[:, :LANES], real[:, LANES:], imag[:, LANES:]
        put(m, 0, *complex_product(gr, gi, f1r, f1i))
        put(m, 1, *conj_product(f0r, f0i, br, bi))
        return carry

    lax.fori_loop(0, 2 * length // TILE, second_body, 0)
    inverse(conv2)

    def last_body(c, carry):
        both = conv2[chunk(c), :]
        second, grad_value = both[:, :LANES], both[:, LANES:]
        staged[0, chunk(c), :] = (gates[1, chunk(c), :] * second).astype(BF16)
        cot[2, offset(c, 0), :] = (og[chunk(c), :].astype(F32) * second).astype(BF16).astype(F32)
        cot[0, offset(c, 0), :] = grad_value.astype(BF16).astype(F32)
        return carry

    lax.fori_loop(0, seq, last_body, 0)
    out_layer = exchange(LAYER, lambda d: staged.at[0, rows(d)], layer_out.at[:, lanes(me)])
    close(2)
    close(0)
    grads_of(2, 3)
    out_two = exchange(SG_TWO, lambda d: staged.at[3, rows(d)], stream_grads.at[2, :, lanes(me)])
    grads_of(0, 1)
    out_value = exchange(SG_VALUE, lambda d: staged.at[1, rows(d)], stream_grads.at[0, :, lanes(me)])
    tap_send[pl.ds(9, 7), :] = jnp.zeros((7, LANES), F32)
    out_taps = exchange(TAPS_OUT, lambda d: tap_send, tap_out.at[:, lanes(me)])
    outs = [out_one, out_layer, out_two, out_value, out_taps]
    for exchanged in outs:
        arrive(exchanged)
    for own, copies in sent + outs:
        for copy in copies:
            copy.wait_send()


def moved(streams, short_taps, long_filters, out_grad):
    seq = lax.axis_size("seq")
    streams_count, part_rows, blocks, channels = streams.shape
    part = part_rows * blocks
    length = part * seq
    fwd, inv = dft_tables(blocks, part_rows * seq)
    any_spec = pl.BlockSpec(memory_space=pl.ANY)
    vmem = pl.BlockSpec(memory_space=pltpu.VMEM)
    flat_taps = jnp.pad(short_taps.reshape(9, channels), ((0, 7), (0, 0)))
    slots = 11
    layer, grads, taps = pl.pallas_call(
        functools.partial(kernel, seq, blocks),
        out_shape=(
            jax.ShapeDtypeStruct((part, channels), BF16),
            jax.ShapeDtypeStruct((3, part, channels), BF16),
            jax.ShapeDtypeStruct((16, channels), F32),
        ),
        in_specs=[any_spec, vmem, any_spec, any_spec, any_spec, any_spec],
        out_specs=(any_spec, any_spec, any_spec),
        scratch_shapes=[
            pltpu.VMEM((2 * length, length), BF16),
            pltpu.VMEM((length, 2 * length), BF16),
            pltpu.VMEM((length, 2 * LANES), BF16),
            pltpu.VMEM((3, length, LANES), BF16),
            pltpu.VMEM((length, LANES), BF16),
            pltpu.VMEM((3, length + 2 * blocks, LANES), F32),
            pltpu.VMEM((3, length + 2 * blocks, LANES), F32),
            pltpu.VMEM((2, length, LANES), F32),
            pltpu.VMEM((length, 2 * LANES), BF16),
            pltpu.VMEM((2 * length, 2 * LANES), F32),
            pltpu.VMEM((2 * length, 2 * LANES), BF16),
            pltpu.VMEM((length, 2 * LANES), F32),
            pltpu.VMEM((length, 2 * LANES), F32),
            pltpu.VMEM((4, length, LANES), BF16),
            pltpu.VMEM((16, LANES), F32),
            pltpu.SemaphoreType.DMA((slots, seq)),
            pltpu.SemaphoreType.DMA((slots, seq)),
            pltpu.SemaphoreType.DMA((2,)),
        ],
        compiler_params=pltpu.CompilerParams(
            collective_id=0, has_side_effects=True, vmem_limit_bytes=48 * 1024 * 1024
        ),
    )(
        streams.reshape(3, part, channels),
        flat_taps,
        long_filters.reshape(2, part, channels),
        out_grad.reshape(part, channels),
        jnp.asarray(fwd),
        jnp.asarray(inv),
    )
    return (
        layer.reshape(part_rows, blocks, channels),
        grads.reshape(3, part_rows, blocks, channels),
        taps[:9].reshape(3, 3, channels),
    )


def either(streams, short_taps, long_filters, out_grad):
    seq = lax.axis_size("seq")
    part_rows, blocks, channels = streams.shape[1:]
    length = part_rows * blocks * seq
    fits = (
        channels == LANES * seq
        and blocks == 8
        and part_rows * blocks % LANES == 0
        and length % TILE == 0
        and length <= 1024
    )
    return (moved if fits else local)(streams, short_taps, long_filters, out_grad)


def solution(mesh):
    in_specs = (
        P(None, "seq", "group", "tensor"),
        P(None, None, "tensor"),
        P(None, "seq", None, "tensor"),
        P("seq", "group", "tensor"),
    )
    out_specs = (
        P("seq", "group", "tensor"),
        P(None, "seq", "group", "tensor"),
        P("group", None, "tensor"),
    )
    return jax.shard_map(either, mesh=mesh, in_specs=in_specs, out_specs=out_specs, check_vma=False)
```

```python
import functools
import math

import jax
import jax.numpy as jnp
import ml_dtypes
import numpy as np
from jax import lax
from jax.experimental import pallas as pl
from jax.experimental.pallas import tpu as pltpu
from jax.sharding import PartitionSpec as P

HIGHEST_PRECISION = lax.Precision.HIGHEST
MESH = pl.DeviceIdType.MESH
LANES = 128
TILE = 256
F32 = jnp.float32
BF16 = jnp.bfloat16


def shifted(value, axis, by):
    count = lax.axis_size(axis)
    return lax.ppermute(value, axis, [(i, (i + by) % count) for i in range(count)])


def complex_product(left_real, left_imag, right_real, right_imag):
    return (
        left_real * right_real - left_imag * right_imag,
        left_real * right_imag + left_imag * right_real,
    )


def conj_product(left_real, left_imag, right_real, right_imag):
    return (
        left_real * right_real + left_imag * right_imag,
        left_real * right_imag - left_imag * right_real,
    )


def local(streams, short_taps, long_filters, out_grad):
    seq_count = lax.axis_size("seq")
    seq_place = lax.axis_index("seq")
    local_rows = streams.shape[1]
    channels = streams.shape[3]
    block_rows = local_rows * seq_count
    full_length = 2 * block_rows * seq_count
    angle_unit = math.pi / full_length
    block_pos = jnp.arange(seq_count, dtype=jnp.int32)
    odd_slots = 2 * block_pos + 1
    local_index = seq_place * local_rows + jnp.arange(local_rows, dtype=jnp.int32)
    row_pos = jnp.arange(block_rows, dtype=jnp.int32)
    start_pos = block_pos[None, :, None] * block_rows + local_index[:, None, None]
    fwd_angle = (start_pos * odd_slots[None, None, :] % (2 * full_length)).astype(
        jnp.float32
    ) * angle_unit
    fwd_table = jnp.stack([jnp.cos(fwd_angle), -jnp.sin(fwd_angle)], axis=-1)
    inner_angle = (row_pos[:, None] * row_pos[None, :] % block_rows).astype(jnp.float32) * (
        2.0 * math.pi / block_rows
    )
    inner_cos = jnp.cos(inner_angle)
    inner_sin = jnp.sin(inner_angle)
    inner_table = jnp.stack(
        [jnp.stack([inner_cos, -inner_sin], axis=-1), jnp.stack([inner_sin, inner_cos], axis=-1)],
        axis=0,
    )
    back_num = (
        row_pos[None, :]
        * (4 * seq_count * row_pos[:, None] + 2 * seq_place + 1)
        % (2 * full_length)
    )
    back_angle = back_num.astype(jnp.float32) * angle_unit
    back_cos = jnp.cos(back_angle)
    back_sin = jnp.sin(back_angle)
    back_table = jnp.stack(
        [jnp.stack([back_cos, back_sin], axis=-1), jnp.stack([-back_sin, back_cos], axis=-1)],
        axis=0,
    )
    outer_angle = (block_pos[:, None] * odd_slots[None, :] % (4 * seq_count)).astype(
        jnp.float32
    ) * (math.pi / (2 * seq_count))
    outer_table = jnp.stack([jnp.cos(outer_angle).T, -jnp.sin(outer_angle).T], axis=0)

    def previous_rows(block):
        edge = shifted(block[:, -1:], "seq", 1)
        rolled = jnp.concatenate([jnp.zeros_like(edge[:, :, :1]), edge[:, :, :-1]], axis=2)
        edge = jnp.where(seq_place == 0, rolled, edge)
        return jnp.concatenate([edge, block[:, :-1]], axis=1)

    def next_rows(block):
        edge = shifted(block[:, :1], "seq", -1)
        rolled = jnp.concatenate([edge[:, :, 1:], jnp.zeros_like(edge[:, :, :1])], axis=2)
        edge = jnp.where(seq_place == seq_count - 1, rolled, edge)
        return jnp.concatenate([block[:, 1:], edge], axis=1)

    def spectra(signals):
        count = signals.shape[0]
        twisted = jnp.einsum("simc,imjr->srijc", signals, fwd_table, precision=HIGHEST_PRECISION)
        slotted = lax.all_to_all(twisted, "seq", split_axis=3, concat_axis=2, tiled=True)
        slotted = slotted.reshape(count, 2, block_rows, channels)
        spec = jnp.einsum("sric,rikq->sqkc", slotted, inner_table, precision=HIGHEST_PRECISION)
        return (spec[:, 0], spec[:, 1])

    def signals_back(real_spec, imag_spec):
        count = real_spec.shape[0]
        stacked = jnp.stack([real_spec, imag_spec], axis=1)
        turned = jnp.einsum("srkc,rkiq->sqic", stacked, back_table, precision=HIGHEST_PRECISION)
        turned = turned.reshape(count, 2, block_rows, 1, channels)
        parts = lax.all_to_all(turned, "seq", split_axis=2, concat_axis=3, tiled=True)
        rows_out = jnp.einsum("srijc,rjm->simc", parts, outer_table, precision=HIGHEST_PRECISION)
        return rows_out * (2.0 / full_length)

    def tap_weight(index):
        return short_taps[:, index][:, None, None, :]

    prev_one = previous_rows(streams)
    prev_two = previous_rows(prev_one)
    filtered = (
        tap_weight(0) * streams + tap_weight(1) * prev_one + tap_weight(2) * prev_two
    ).astype(jnp.bfloat16)
    value_stream = filtered[0].astype(jnp.float32)
    gate_one = filtered[1].astype(jnp.float32)
    gate_two = filtered[2].astype(jnp.float32)
    filters = long_filters.astype(jnp.float32)
    real_first, imag_first = spectra(jnp.stack([value_stream, filters[0]]))
    product_one = complex_product(real_first[0], imag_first[0], real_first[1], imag_first[1])
    first_conv = signals_back(product_one[0][None], product_one[1][None])[0]
    gated_first = gate_one * first_conv
    real_second, imag_second = spectra(jnp.stack([gated_first, filters[1]]))
    product_two = complex_product(real_second[0], imag_second[0], real_second[1], imag_second[1])
    second_conv = signals_back(product_two[0][None], product_two[1][None])[0]
    layer_out = (gate_two * second_conv).astype(jnp.bfloat16)
    cotangent = out_grad.astype(jnp.float32)
    back_two = cotangent * gate_two
    grad_two = cotangent * second_conv
    real_third, imag_third = spectra(back_two[None])
    filter_two_real, filter_two_imag = (real_second[1], imag_second[1])
    correlated_two = conj_product(filter_two_real, filter_two_imag, real_third[0], imag_third[0])
    grad_gated = signals_back(correlated_two[0][None], correlated_two[1][None])[0]
    grad_one = grad_gated * first_conv
    back_one = grad_gated * gate_one
    real_fourth, imag_fourth = spectra(back_one[None])
    filter_one_real, filter_one_imag = (real_first[1], imag_first[1])
    correlated_one = conj_product(filter_one_real, filter_one_imag, real_fourth[0], imag_fourth[0])
    grad_value = signals_back(correlated_one[0][None], correlated_one[1][None])[0]
    stream_cot = jnp.stack([grad_value, grad_one, grad_two]).astype(jnp.bfloat16)
    next_one = next_rows(stream_cot)
    next_two = next_rows(next_one)
    stream_grads = (
        tap_weight(0) * stream_cot + tap_weight(1) * next_one + tap_weight(2) * next_two
    ).astype(jnp.bfloat16)
    cot_float = stream_cot.astype(jnp.float32)
    tap_terms = jnp.stack(
        [
            jnp.sum(cot_float * streams, axis=(1, 2)),
            jnp.sum(cot_float * prev_one, axis=(1, 2)),
            jnp.sum(cot_float * prev_two, axis=(1, 2)),
        ],
        axis=1,
    )
    tap_total = lax.psum(tap_terms, "seq")
    return (layer_out, stream_grads, tap_total * (1.0 / math.sqrt(block_rows * seq_count)))


def split_table(table):
    high = table.astype(ml_dtypes.bfloat16)
    low = (table - high.astype(np.float64)).astype(ml_dtypes.bfloat16)
    return np.stack([high, low])


def dft_tables(blocks, rows):
    length = blocks * rows
    place = np.arange(length)
    time = (place % blocks) * rows + place // blocks
    half = TILE // 2
    freq = np.arange(length).reshape(-1, half)
    angle = ((2 * freq[:, :, None] + 1) * time[None, None, :] % (4 * length)) * (math.pi / (2 * length))
    table = np.concatenate([np.cos(angle), -np.sin(angle)], axis=1).reshape(2 * length, length)
    return split_table(table), split_table(table.T / length)


FILTER0, FILTER1, VALUE, GATE_TWO, OUT_GRAD, GATE_ONE, SG_ONE, LAYER, SG_TWO, SG_VALUE, TAPS_OUT = range(11)


def kernel(
    seq, blocks, streams, taps, filters, out_grad, fwd_hbm, inv_hbm,
    layer_out, stream_grads, tap_out,
    fwd, inv, xf, sb, og, s32, cot, gates, sig, sig_low, spec_f, prod, prod_low, conv, conv2, staged, tap_send,
    send_sem, recv_sem, table_sem,
):
    me = lax.axis_index("seq")
    group = lax.axis_index("group")
    other = 1 - group
    part = streams.shape[1]
    length = part * seq
    half = TILE // 2
    order = sorted(range(1, seq), key=lambda k: abs(k - seq / 2))

    def peer(k):
        return lax.rem(me + k, seq)

    def lanes(d):
        return pl.ds(pl.multiple_of(d * LANES, LANES), LANES)

    def rows(d):
        return pl.ds(pl.multiple_of(d * part, part), part)

    def remote(slot, k, src, dst):
        return pltpu.make_async_remote_copy(
            src_ref=src, dst_ref=dst, send_sem=send_sem.at[slot, k], recv_sem=recv_sem.at[slot, k],
            device_id={"seq": peer(k)}, device_id_type=MESH,
        )

    def exchange(slot, src_of, dst):
        own = pltpu.make_async_copy(src_of(me), dst, recv_sem.at[slot, 0])
        copies = [remote(slot, k, src_of(peer(k)), dst) for k in order]
        for copy in copies:
            copy.start()
        own.start()
        return own, copies

    def arrive(exchanged):
        own, copies = exchanged
        own.wait()
        for copy in copies:
            copy.wait_recv()

    barrier = pltpu.get_barrier_semaphore()
    for k in range(1, seq):
        pl.semaphore_signal(barrier, inc=1, device_id={"seq": peer(k)}, device_id_type=MESH)
    pl.semaphore_signal(barrier, inc=1, device_id={"group": other}, device_id_type=MESH)
    fwd_copy = pltpu.make_async_copy(fwd_hbm, fwd, table_sem.at[0])
    inv_copy = pltpu.make_async_copy(inv_hbm, inv, table_sem.at[1])
    pl.semaphore_wait(barrier, seq)

    mine = rows(me)
    in_f = exchange(FILTER0, lambda d: filters.at[group, :, lanes(d)], xf.at[mine, lanes(group)])
    own_f1 = pltpu.make_async_copy(
        filters.at[other, :, lanes(me)], xf.at[mine, lanes(other)], recv_sem.at[FILTER1, 0]
    )
    own_f1.start()
    fwd_copy.start()
    in_v = exchange(VALUE, lambda d: streams.at[0, :, lanes(d)], sb.at[0, mine])
    in_g2 = exchange(GATE_TWO, lambda d: streams.at[2, :, lanes(d)], sb.at[2, mine])
    in_og = exchange(OUT_GRAD, lambda d: out_grad.at[:, lanes(d)], og.at[mine])
    in_g1 = exchange(GATE_ONE, lambda d: streams.at[1, :, lanes(d)], sb.at[1, mine])
    inv_copy.start()
    sent = [in_f, in_v, in_g2, in_og, in_g1]

    pad = 2 * blocks
    sub = lax.broadcasted_iota(jnp.int32, (blocks, LANES), 0)

    def tap(s, j):
        return taps[s, pl.ds(j, 1), lanes(me)]

    def chunk(c):
        return pl.ds(pl.multiple_of(c * part, part), part)

    def offset(c, by):
        return pl.ds(pl.multiple_of(c * part + by, blocks), part)

    def widen(s):
        def body(c, carry):
            s32[s, offset(c, pad), :] = sb[s, chunk(c), :].astype(F32)
            return carry

        lax.fori_loop(0, seq, body, 0)
        for step in range(2):
            edge = s32[s, pl.ds(length + step * blocks, blocks), :]
            s32[s, pl.ds(step * blocks, blocks), :] = jnp.where(sub == 0, 0.0, pltpu.roll(edge, 1, 0))

    def filtered(s, c):
        total = tap(s, 0) * s32[s, offset(c, pad), :]
        total = total + tap(s, 1) * s32[s, offset(c, blocks), :]
        total = total + tap(s, 2) * s32[s, offset(c, 0), :]
        return total.astype(BF16)

    def cots(s, c):
        base = [cot[s, offset(c, j * blocks), :] for j in range(3)]
        total = tap(s, 0) * base[0] + tap(s, 1) * base[1] + tap(s, 2) * base[2]
        return total.astype(BF16)

    def close(s):
        for step in range(2):
            edge = cot[s, pl.ds(step * blocks, blocks), :]
            cot[s, pl.ds(length + step * blocks, blocks), :] = jnp.where(
                sub == blocks - 1, 0.0, pltpu.roll(edge, blocks - 1, 0)
            )

    def grads_of(s, slot):
        def body(c, carry):
            staged[slot, chunk(c), :] = cots(s, c)
            return carry

        lax.fori_loop(0, seq, body, 0)

    def taps_of(s):
        def body(c, sums):
            now = cot[s, offset(c, 0), :]
            return tuple(
                sums[j]
                + jnp.sum(
                    (now * s32[s, offset(c, pad - j * blocks), :]).reshape(-1, 8, LANES), axis=0
                )
                for j in range(3)
            )

        sums = lax.fori_loop(0, seq, body, tuple(jnp.zeros((8, LANES), F32) for _ in range(3)))
        for j in range(3):
            tap_send[s, pl.ds(j, 1), :] = jnp.sum(sums[j], axis=0, keepdims=True) * (
                1.0 / math.sqrt(length)
            )

    def tile(m):
        return pl.ds(pl.multiple_of(m * TILE, TILE), TILE)

    def forward(m, signals):
        out = jnp.dot(fwd[0, tile(m), :], signals[...], preferred_element_type=F32)
        return out[:half], out[half:]

    def put(m, col, real, imag):
        prod[pl.ds(pl.multiple_of(m * TILE, TILE), half), col * LANES:(col + 1) * LANES] = real.astype(BF16)
        prod[pl.ds(pl.multiple_of(m * TILE + half, half), half), col * LANES:(col + 1) * LANES] = imag.astype(BF16)

    def spectra_of(m, col):
        cols = slice(col * LANES, (col + 1) * LANES)
        return (
            spec_f[pl.ds(pl.multiple_of(m * TILE, TILE), half), cols],
            spec_f[pl.ds(pl.multiple_of(m * TILE + half, half), half), cols],
        )

    def put_low(m, col, real, imag):
        for start, value in ((0, real), (half, imag)):
            low = (value - value.astype(BF16).astype(F32)).astype(BF16)
            prod_low[pl.ds(pl.multiple_of(m * TILE + start, half), half), col * LANES:(col + 1) * LANES] = low

    def inverse(into, split):
        def body(m, carry):
            out = jnp.dot(inv[0, tile(m), :], prod[...], preferred_element_type=F32)
            if split:
                out = out + jnp.dot(inv[1, tile(m), :], prod[...], preferred_element_type=F32)
                out = out + jnp.dot(inv[0, tile(m), :], prod_low[...], preferred_element_type=F32)
            into[tile(m), :] = out
            return carry

        lax.fori_loop(0, length // TILE, body, 0)

    in_f[0].wait()
    handed = []
    for k, copy in zip(order, in_f[1]):
        copy.wait_recv()
        piece = xf.at[rows(lax.rem(me - k + seq, seq)), lanes(group)]
        hand = pltpu.make_async_remote_copy(
            src_ref=piece, dst_ref=piece, send_sem=send_sem.at[FILTER1, k],
            recv_sem=recv_sem.at[FILTER1, k], device_id={"group": other}, device_id_type=MESH,
        )
        hand.start()
        handed.append(hand)
    sent.append((own_f1, handed))
    arrive((own_f1, handed))
    fwd_copy.wait()

    def filter_body(m, carry):
        out = jnp.dot(fwd[0, tile(m), :], xf[...], preferred_element_type=F32)
        spec_f[tile(m), :] = out + jnp.dot(fwd[1, tile(m), :], xf[...], preferred_element_type=F32)
        return carry

    lax.fori_loop(0, 2 * length // TILE, filter_body, 0)

    arrive(in_v)
    widen(0)

    def value_body(c, carry):
        sig[chunk(c), 0:LANES] = filtered(0, c)
        return carry

    lax.fori_loop(0, seq, value_body, 0)
    arrive(in_g2)
    widen(2)

    arrive(in_og)

    def back_body(c, carry):
        gate = filtered(2, c)
        gates[1, chunk(c), :] = gate.astype(F32)
        back = og[chunk(c), :].astype(F32) * gate.astype(F32)
        sig[chunk(c), LANES:] = back.astype(BF16)
        sig_low[chunk(c), :] = (back - back.astype(BF16).astype(F32)).astype(BF16)
        return carry

    lax.fori_loop(0, seq, back_body, 0)

    def first_body(m, carry):
        out = jnp.dot(fwd[0, tile(m), :], sig[...], preferred_element_type=F32)
        out = out + jnp.dot(fwd[1, tile(m), :], sig[...], preferred_element_type=F32)
        low = jnp.dot(fwd[0, tile(m), :], sig_low[...], preferred_element_type=F32)
        back = out[:, LANES:] + low
        f0r, f0i = spectra_of(m, 0)
        f1r, f1i = spectra_of(m, 1)
        first = complex_product(out[:half, :LANES], out[half:, :LANES], f0r, f0i)
        second = conj_product(f1r, f1i, back[:half], back[half:])
        put(m, 0, *first)
        put_low(m, 0, *first)
        put(m, 1, *second)
        put_low(m, 1, *second)
        return carry

    lax.fori_loop(0, 2 * length // TILE, first_body, 0)
    inv_copy.wait()
    inverse(conv, True)

    def one_body(c, carry):
        both = conv[chunk(c), :]
        cot[1, offset(c, 0), :] = (both[:, LANES:] * both[:, :LANES]).astype(BF16).astype(F32)
        return carry

    lax.fori_loop(0, seq, one_body, 0)
    close(1)
    grads_of(1, 2)
    out_one = exchange(SG_ONE, lambda d: staged.at[2, rows(d)], stream_grads.at[1, :, lanes(me)])
    arrive(in_g1)
    widen(1)

    def gated_body(c, carry):
        gate = filtered(1, c).astype(F32)
        both = conv[chunk(c), :]
        sig[chunk(c), 0:LANES] = (gate * both[:, :LANES]).astype(BF16)
        sig[chunk(c), LANES:] = (gate * both[:, LANES:]).astype(BF16)
        return carry

    lax.fori_loop(0, seq, gated_body, 0)

    def second_body(m, carry):
        real, imag = forward(m, sig)
        f0r, f0i = spectra_of(m, 0)
        f1r, f1i = spectra_of(m, 1)
        gr, gi, br, bi = real[:, :LANES], imag[:, :LANES], real[:, LANES:], imag[:, LANES:]
        put(m, 0, *complex_product(gr, gi, f1r, f1i))
        put(m, 1, *conj_product(f0r, f0i, br, bi))
        return carry

    lax.fori_loop(0, 2 * length // TILE, second_body, 0)
    inverse(conv2, False)

    def last_body(c, carry):
        both = conv2[chunk(c), :]
        second, grad_value = both[:, :LANES], both[:, LANES:]
        staged[0, chunk(c), :] = (gates[1, chunk(c), :] * second).astype(BF16)
        cot[2, offset(c, 0), :] = (og[chunk(c), :].astype(F32) * second).astype(BF16).astype(F32)
        cot[0, offset(c, 0), :] = grad_value.astype(BF16).astype(F32)
        return carry

    lax.fori_loop(0, seq, last_body, 0)
    out_layer = exchange(LAYER, lambda d: staged.at[0, rows(d)], layer_out.at[:, lanes(me)])
    close(2)
    close(0)
    grads_of(2, 3)
    out_two = exchange(SG_TWO, lambda d: staged.at[3, rows(d)], stream_grads.at[2, :, lanes(me)])
    grads_of(0, 1)
    out_value = exchange(SG_VALUE, lambda d: staged.at[1, rows(d)], stream_grads.at[0, :, lanes(me)])
    for s in range(3):
        taps_of(s)
    out_taps = exchange(TAPS_OUT, lambda d: tap_send, tap_out.at[:, :, lanes(me)])
    outs = [out_one, out_layer, out_two, out_value, out_taps]
    for exchanged in outs:
        arrive(exchanged)
    for own, copies in sent + outs:
        for copy in copies:
            copy.wait_send()


def moved(streams, short_taps, long_filters, out_grad):
    seq = lax.axis_size("seq")
    streams_count, part_rows, blocks, channels = streams.shape
    part = part_rows * blocks
    length = part * seq
    fwd, inv = dft_tables(blocks, part_rows * seq)
    any_spec = pl.BlockSpec(memory_space=pl.ANY)
    hbm = pl.BlockSpec(memory_space=pltpu.HBM)
    vmem = pl.BlockSpec(memory_space=pltpu.VMEM)
    slots = 11
    layer, grads, taps = pl.pallas_call(
        functools.partial(kernel, seq, blocks),
        out_shape=(
            jax.ShapeDtypeStruct((part, channels), BF16),
            jax.ShapeDtypeStruct((3, part, channels), BF16),
            jax.ShapeDtypeStruct((3, 3, channels), F32),
        ),
        in_specs=[hbm, vmem, hbm, hbm, hbm, hbm],
        out_specs=(any_spec, any_spec, any_spec),
        scratch_shapes=[
            pltpu.VMEM((2, 2 * length, length), BF16),
            pltpu.VMEM((2, length, 2 * length), BF16),
            pltpu.VMEM((length, 2 * LANES), BF16),
            pltpu.VMEM((3, length, LANES), BF16),
            pltpu.VMEM((length, LANES), BF16),
            pltpu.VMEM((3, length + 2 * blocks, LANES), F32),
            pltpu.VMEM((3, length + 2 * blocks, LANES), F32),
            pltpu.VMEM((2, length, LANES), F32),
            pltpu.VMEM((length, 2 * LANES), BF16),
            pltpu.VMEM((length, LANES), BF16),
            pltpu.VMEM((2 * length, 2 * LANES), F32),
            pltpu.VMEM((2 * length, 2 * LANES), BF16),
            pltpu.VMEM((2 * length, 2 * LANES), BF16),
            pltpu.VMEM((length, 2 * LANES), F32),
            pltpu.VMEM((length, 2 * LANES), F32),
            pltpu.VMEM((4, length, LANES), BF16),
            pltpu.VMEM((3, 3, LANES), F32),
            pltpu.SemaphoreType.DMA((slots, seq)),
            pltpu.SemaphoreType.DMA((slots, seq)),
            pltpu.SemaphoreType.DMA((2,)),
        ],
        compiler_params=pltpu.CompilerParams(
            collective_id=0, has_side_effects=True, vmem_limit_bytes=48 * 1024 * 1024
        ),
    )(
        streams.reshape(3, part, channels),
        short_taps,
        long_filters.reshape(2, part, channels),
        out_grad.reshape(part, channels),
        jnp.asarray(fwd),
        jnp.asarray(inv),
    )
    return (
        layer.reshape(part_rows, blocks, channels),
        grads.reshape(3, part_rows, blocks, channels),
        taps,
    )


def either(streams, short_taps, long_filters, out_grad):
    seq = lax.axis_size("seq")
    part_rows, blocks, channels = streams.shape[1:]
    length = part_rows * blocks * seq
    fits = (
        channels == LANES * seq
        and lax.axis_size("group") == 2
        and blocks == 8
        and part_rows * blocks % LANES == 0
        and length % TILE == 0
        and length <= 1024
    )
    return (moved if fits else local)(streams, short_taps, long_filters, out_grad)


def solution(mesh):
    in_specs = (
        P(None, "seq", "group", "tensor"),
        P(None, None, "tensor"),
        P(None, "seq", None, "tensor"),
        P("seq", "group", "tensor"),
    )
    out_specs = (
        P("seq", "group", "tensor"),
        P(None, "seq", "group", "tensor"),
        P("group", None, "tensor"),
    )
    return jax.shard_map(either, mesh=mesh, in_specs=in_specs, out_specs=out_specs, check_vma=False)
```

```python
import functools
import math

import jax
import jax.numpy as jnp
import ml_dtypes
import numpy as np
from jax import lax
from jax.experimental import pallas as pl
from jax.experimental.pallas import tpu as pltpu
from jax.sharding import PartitionSpec as P

HIGHEST_PRECISION = lax.Precision.HIGHEST
MESH = pl.DeviceIdType.MESH
LANES = 128
TILE = 256
F32 = jnp.float32
BF16 = jnp.bfloat16


def shifted(value, axis, by):
    count = lax.axis_size(axis)
    return lax.ppermute(value, axis, [(i, (i + by) % count) for i in range(count)])


def complex_product(left_real, left_imag, right_real, right_imag):
    return (
        left_real * right_real - left_imag * right_imag,
        left_real * right_imag + left_imag * right_real,
    )


def conj_product(left_real, left_imag, right_real, right_imag):
    return (
        left_real * right_real + left_imag * right_imag,
        left_real * right_imag - left_imag * right_real,
    )


def local(streams, short_taps, long_filters, out_grad):
    seq_count = lax.axis_size("seq")
    seq_place = lax.axis_index("seq")
    local_rows = streams.shape[1]
    channels = streams.shape[3]
    block_rows = local_rows * seq_count
    full_length = 2 * block_rows * seq_count
    angle_unit = math.pi / full_length
    block_pos = jnp.arange(seq_count, dtype=jnp.int32)
    odd_slots = 2 * block_pos + 1
    local_index = seq_place * local_rows + jnp.arange(local_rows, dtype=jnp.int32)
    row_pos = jnp.arange(block_rows, dtype=jnp.int32)
    start_pos = block_pos[None, :, None] * block_rows + local_index[:, None, None]
    fwd_angle = (start_pos * odd_slots[None, None, :] % (2 * full_length)).astype(
        jnp.float32
    ) * angle_unit
    fwd_table = jnp.stack([jnp.cos(fwd_angle), -jnp.sin(fwd_angle)], axis=-1)
    inner_angle = (row_pos[:, None] * row_pos[None, :] % block_rows).astype(jnp.float32) * (
        2.0 * math.pi / block_rows
    )
    inner_cos = jnp.cos(inner_angle)
    inner_sin = jnp.sin(inner_angle)
    inner_table = jnp.stack(
        [jnp.stack([inner_cos, -inner_sin], axis=-1), jnp.stack([inner_sin, inner_cos], axis=-1)],
        axis=0,
    )
    back_num = (
        row_pos[None, :]
        * (4 * seq_count * row_pos[:, None] + 2 * seq_place + 1)
        % (2 * full_length)
    )
    back_angle = back_num.astype(jnp.float32) * angle_unit
    back_cos = jnp.cos(back_angle)
    back_sin = jnp.sin(back_angle)
    back_table = jnp.stack(
        [jnp.stack([back_cos, back_sin], axis=-1), jnp.stack([-back_sin, back_cos], axis=-1)],
        axis=0,
    )
    outer_angle = (block_pos[:, None] * odd_slots[None, :] % (4 * seq_count)).astype(
        jnp.float32
    ) * (math.pi / (2 * seq_count))
    outer_table = jnp.stack([jnp.cos(outer_angle).T, -jnp.sin(outer_angle).T], axis=0)

    def previous_rows(block):
        edge = shifted(block[:, -1:], "seq", 1)
        rolled = jnp.concatenate([jnp.zeros_like(edge[:, :, :1]), edge[:, :, :-1]], axis=2)
        edge = jnp.where(seq_place == 0, rolled, edge)
        return jnp.concatenate([edge, block[:, :-1]], axis=1)

    def next_rows(block):
        edge = shifted(block[:, :1], "seq", -1)
        rolled = jnp.concatenate([edge[:, :, 1:], jnp.zeros_like(edge[:, :, :1])], axis=2)
        edge = jnp.where(seq_place == seq_count - 1, rolled, edge)
        return jnp.concatenate([block[:, 1:], edge], axis=1)

    def spectra(signals):
        count = signals.shape[0]
        twisted = jnp.einsum("simc,imjr->srijc", signals, fwd_table, precision=HIGHEST_PRECISION)
        slotted = lax.all_to_all(twisted, "seq", split_axis=3, concat_axis=2, tiled=True)
        slotted = slotted.reshape(count, 2, block_rows, channels)
        spec = jnp.einsum("sric,rikq->sqkc", slotted, inner_table, precision=HIGHEST_PRECISION)
        return (spec[:, 0], spec[:, 1])

    def signals_back(real_spec, imag_spec):
        count = real_spec.shape[0]
        stacked = jnp.stack([real_spec, imag_spec], axis=1)
        turned = jnp.einsum("srkc,rkiq->sqic", stacked, back_table, precision=HIGHEST_PRECISION)
        turned = turned.reshape(count, 2, block_rows, 1, channels)
        parts = lax.all_to_all(turned, "seq", split_axis=2, concat_axis=3, tiled=True)
        rows_out = jnp.einsum("srijc,rjm->simc", parts, outer_table, precision=HIGHEST_PRECISION)
        return rows_out * (2.0 / full_length)

    def tap_weight(index):
        return short_taps[:, index][:, None, None, :]

    prev_one = previous_rows(streams)
    prev_two = previous_rows(prev_one)
    filtered = (
        tap_weight(0) * streams + tap_weight(1) * prev_one + tap_weight(2) * prev_two
    ).astype(jnp.bfloat16)
    value_stream = filtered[0].astype(jnp.float32)
    gate_one = filtered[1].astype(jnp.float32)
    gate_two = filtered[2].astype(jnp.float32)
    filters = long_filters.astype(jnp.float32)
    real_first, imag_first = spectra(jnp.stack([value_stream, filters[0]]))
    product_one = complex_product(real_first[0], imag_first[0], real_first[1], imag_first[1])
    first_conv = signals_back(product_one[0][None], product_one[1][None])[0]
    gated_first = gate_one * first_conv
    real_second, imag_second = spectra(jnp.stack([gated_first, filters[1]]))
    product_two = complex_product(real_second[0], imag_second[0], real_second[1], imag_second[1])
    second_conv = signals_back(product_two[0][None], product_two[1][None])[0]
    layer_out = (gate_two * second_conv).astype(jnp.bfloat16)
    cotangent = out_grad.astype(jnp.float32)
    back_two = cotangent * gate_two
    grad_two = cotangent * second_conv
    real_third, imag_third = spectra(back_two[None])
    filter_two_real, filter_two_imag = (real_second[1], imag_second[1])
    correlated_two = conj_product(filter_two_real, filter_two_imag, real_third[0], imag_third[0])
    grad_gated = signals_back(correlated_two[0][None], correlated_two[1][None])[0]
    grad_one = grad_gated * first_conv
    back_one = grad_gated * gate_one
    real_fourth, imag_fourth = spectra(back_one[None])
    filter_one_real, filter_one_imag = (real_first[1], imag_first[1])
    correlated_one = conj_product(filter_one_real, filter_one_imag, real_fourth[0], imag_fourth[0])
    grad_value = signals_back(correlated_one[0][None], correlated_one[1][None])[0]
    stream_cot = jnp.stack([grad_value, grad_one, grad_two]).astype(jnp.bfloat16)
    next_one = next_rows(stream_cot)
    next_two = next_rows(next_one)
    stream_grads = (
        tap_weight(0) * stream_cot + tap_weight(1) * next_one + tap_weight(2) * next_two
    ).astype(jnp.bfloat16)
    cot_float = stream_cot.astype(jnp.float32)
    tap_terms = jnp.stack(
        [
            jnp.sum(cot_float * streams, axis=(1, 2)),
            jnp.sum(cot_float * prev_one, axis=(1, 2)),
            jnp.sum(cot_float * prev_two, axis=(1, 2)),
        ],
        axis=1,
    )
    tap_total = lax.psum(tap_terms, "seq")
    return (layer_out, stream_grads, tap_total * (1.0 / math.sqrt(block_rows * seq_count)))


def split_table(table):
    high = table.astype(ml_dtypes.bfloat16)
    low = (table - high.astype(np.float64)).astype(ml_dtypes.bfloat16)
    return np.stack([high, low])


def dft_tables(blocks, rows):
    length = blocks * rows
    place = np.arange(length)
    time = (place % blocks) * rows + place // blocks
    half = TILE // 2
    freq = np.arange(length).reshape(-1, half)
    angle = ((2 * freq[:, :, None] + 1) * time[None, None, :] % (4 * length)) * (math.pi / (2 * length))
    table = np.concatenate([np.cos(angle), -np.sin(angle)], axis=1).reshape(2 * length, length)
    return split_table(table), split_table(table.T / length)


FILTER0, FILTER1, VALUE, GATE_TWO, OUT_GRAD, GATE_ONE, SG_ONE, LAYER, SG_TWO, SG_VALUE, TAPS_OUT = range(11)


def kernel(
    seq, blocks, streams, taps, filters, out_grad, fwd_hbm, inv_hbm,
    layer_out, stream_grads, tap_out,
    fwd, inv, xf, sb, og, s32, cot, gates, sig, sig_low, spec_f, prod, conv, conv2, staged, tap_send,
    send_sem, recv_sem, table_sem,
):
    me = lax.axis_index("seq")
    group = lax.axis_index("group")
    other = 1 - group
    part = streams.shape[1]
    length = part * seq
    half = TILE // 2
    order = sorted(range(1, seq), key=lambda k: abs(k - seq / 2))

    def peer(k):
        return lax.rem(me + k, seq)

    def lanes(d):
        return pl.ds(pl.multiple_of(d * LANES, LANES), LANES)

    def rows(d):
        return pl.ds(pl.multiple_of(d * part, part), part)

    def remote(slot, k, src, dst):
        return pltpu.make_async_remote_copy(
            src_ref=src, dst_ref=dst, send_sem=send_sem.at[slot, k], recv_sem=recv_sem.at[slot, k],
            device_id={"seq": peer(k)}, device_id_type=MESH,
        )

    def exchange(slot, src_of, dst):
        own = pltpu.make_async_copy(src_of(me), dst, recv_sem.at[slot, 0])
        copies = [remote(slot, k, src_of(peer(k)), dst) for k in order]
        for copy in copies:
            copy.start()
        own.start()
        return own, copies

    def arrive(exchanged):
        own, copies = exchanged
        own.wait()
        for copy in copies:
            copy.wait_recv()

    barrier = pltpu.get_barrier_semaphore()
    for k in range(1, seq):
        pl.semaphore_signal(barrier, inc=1, device_id={"seq": peer(k)}, device_id_type=MESH)
    pl.semaphore_signal(barrier, inc=1, device_id={"group": other}, device_id_type=MESH)
    fwd_copy = pltpu.make_async_copy(fwd_hbm, fwd, table_sem.at[0])
    inv_copy = pltpu.make_async_copy(inv_hbm, inv, table_sem.at[1])
    pl.semaphore_wait(barrier, seq)

    mine = rows(me)
    in_f = exchange(FILTER0, lambda d: filters.at[group, :, lanes(d)], xf.at[mine, lanes(group)])
    own_f1 = pltpu.make_async_copy(
        filters.at[other, :, lanes(me)], xf.at[mine, lanes(other)], recv_sem.at[FILTER1, 0]
    )
    own_f1.start()
    fwd_copy.start()
    in_v = exchange(VALUE, lambda d: streams.at[0, :, lanes(d)], sb.at[0, mine])
    in_g2 = exchange(GATE_TWO, lambda d: streams.at[2, :, lanes(d)], sb.at[2, mine])
    in_og = exchange(OUT_GRAD, lambda d: out_grad.at[:, lanes(d)], og.at[mine])
    in_g1 = exchange(GATE_ONE, lambda d: streams.at[1, :, lanes(d)], sb.at[1, mine])
    inv_copy.start()
    sent = [in_f, in_v, in_g2, in_og, in_g1]

    pad = 2 * blocks
    sub = lax.broadcasted_iota(jnp.int32, (blocks, LANES), 0)

    def tap(s, j):
        return taps[s, pl.ds(j, 1), lanes(me)]

    def chunk(c):
        return pl.ds(pl.multiple_of(c * part, part), part)

    def offset(c, by):
        return pl.ds(pl.multiple_of(c * part + by, blocks), part)

    def widen(s):
        def body(c, carry):
            s32[s, offset(c, pad), :] = sb[s, chunk(c), :].astype(F32)
            return carry

        lax.fori_loop(0, seq, body, 0)
        for step in range(2):
            edge = s32[s, pl.ds(length + step * blocks, blocks), :]
            s32[s, pl.ds(step * blocks, blocks), :] = jnp.where(sub == 0, 0.0, pltpu.roll(edge, 1, 0))

    def filtered(s, c):
        total = tap(s, 0) * s32[s, offset(c, pad), :]
        total = total + tap(s, 1) * s32[s, offset(c, blocks), :]
        total = total + tap(s, 2) * s32[s, offset(c, 0), :]
        return total.astype(BF16)

    def cots(s, c):
        base = [cot[s, offset(c, j * blocks), :] for j in range(3)]
        total = tap(s, 0) * base[0] + tap(s, 1) * base[1] + tap(s, 2) * base[2]
        return total.astype(BF16)

    def close(s):
        for step in range(2):
            edge = cot[s, pl.ds(step * blocks, blocks), :]
            cot[s, pl.ds(length + step * blocks, blocks), :] = jnp.where(
                sub == blocks - 1, 0.0, pltpu.roll(edge, blocks - 1, 0)
            )

    def grads_of(s, slot):
        def body(c, carry):
            staged[slot, chunk(c), :] = cots(s, c)
            return carry

        lax.fori_loop(0, seq, body, 0)

    def taps_of(s):
        def body(c, sums):
            now = cot[s, offset(c, 0), :]
            return tuple(
                sums[j]
                + jnp.sum(
                    (now * s32[s, offset(c, pad - j * blocks), :]).reshape(-1, 8, LANES), axis=0
                )
                for j in range(3)
            )

        sums = lax.fori_loop(0, seq, body, tuple(jnp.zeros((8, LANES), F32) for _ in range(3)))
        for j in range(3):
            tap_send[s, pl.ds(j, 1), :] = jnp.sum(sums[j], axis=0, keepdims=True) * (
                1.0 / math.sqrt(length)
            )

    def tile(m):
        return pl.ds(pl.multiple_of(m * TILE, TILE), TILE)

    def forward(m, signals):
        out = jnp.dot(fwd[0, tile(m), :], signals[...], preferred_element_type=F32)
        return out[:half], out[half:]

    def put(m, col, real, imag):
        prod[pl.ds(pl.multiple_of(m * TILE, TILE), half), col * LANES:(col + 1) * LANES] = real.astype(BF16)
        prod[pl.ds(pl.multiple_of(m * TILE + half, half), half), col * LANES:(col + 1) * LANES] = imag.astype(BF16)

    def spectra_of(m, col):
        cols = slice(col * LANES, (col + 1) * LANES)
        return (
            spec_f[pl.ds(pl.multiple_of(m * TILE, TILE), half), cols],
            spec_f[pl.ds(pl.multiple_of(m * TILE + half, half), half), cols],
        )

    def inverse(into, split):
        def body(m, carry):
            out = jnp.dot(inv[0, tile(m), :], prod[...], preferred_element_type=F32)
            if split:
                out = out + jnp.dot(inv[1, tile(m), :], prod[...], preferred_element_type=F32)
            into[tile(m), :] = out
            return carry

        lax.fori_loop(0, length // TILE, body, 0)

    in_f[0].wait()
    handed = []
    for k, copy in zip(order, in_f[1]):
        copy.wait_recv()
        piece = xf.at[rows(lax.rem(me - k + seq, seq)), lanes(group)]
        hand = pltpu.make_async_remote_copy(
            src_ref=piece, dst_ref=piece, send_sem=send_sem.at[FILTER1, k],
            recv_sem=recv_sem.at[FILTER1, k], device_id={"group": other}, device_id_type=MESH,
        )
        hand.start()
        handed.append(hand)
    sent.append((own_f1, handed))
    arrive((own_f1, handed))
    fwd_copy.wait()

    def filter_body(m, carry):
        out = jnp.dot(fwd[0, tile(m), :], xf[...], preferred_element_type=F32)
        spec_f[tile(m), :] = out + jnp.dot(fwd[1, tile(m), :], xf[...], preferred_element_type=F32)
        return carry

    lax.fori_loop(0, 2 * length // TILE, filter_body, 0)

    arrive(in_v)
    widen(0)

    def value_body(c, carry):
        sig[chunk(c), 0:LANES] = filtered(0, c)
        return carry

    lax.fori_loop(0, seq, value_body, 0)
    arrive(in_g2)
    widen(2)

    arrive(in_og)

    def back_body(c, carry):
        gate = filtered(2, c)
        gates[1, chunk(c), :] = gate.astype(F32)
        back = og[chunk(c), :].astype(F32) * gate.astype(F32)
        sig[chunk(c), LANES:] = back.astype(BF16)
        sig_low[chunk(c), :] = (back - back.astype(BF16).astype(F32)).astype(BF16)
        return carry

    lax.fori_loop(0, seq, back_body, 0)

    def first_body(m, carry):
        out = jnp.dot(fwd[0, tile(m), :], sig[...], preferred_element_type=F32)
        out = out + jnp.dot(fwd[1, tile(m), :], sig[...], preferred_element_type=F32)
        low = jnp.dot(fwd[0, tile(m), :], sig_low[...], preferred_element_type=F32)
        back = out[:, LANES:] + low
        f0r, f0i = spectra_of(m, 0)
        f1r, f1i = spectra_of(m, 1)
        first = complex_product(out[:half, :LANES], out[half:, :LANES], f0r, f0i)
        second = conj_product(f1r, f1i, back[:half], back[half:])
        put(m, 0, *first)
        put(m, 1, *second)
        return carry

    lax.fori_loop(0, 2 * length // TILE, first_body, 0)
    inv_copy.wait()
    inverse(conv, True)

    def one_body(c, carry):
        both = conv[chunk(c), :]
        cot[1, offset(c, 0), :] = (both[:, LANES:] * both[:, :LANES]).astype(BF16).astype(F32)
        return carry

    lax.fori_loop(0, seq, one_body, 0)
    close(1)
    grads_of(1, 2)
    out_one = exchange(SG_ONE, lambda d: staged.at[2, rows(d)], stream_grads.at[1, :, lanes(me)])
    arrive(in_g1)
    widen(1)

    def gated_body(c, carry):
        gate = filtered(1, c).astype(F32)
        both = conv[chunk(c), :]
        sig[chunk(c), 0:LANES] = (gate * both[:, :LANES]).astype(BF16)
        sig[chunk(c), LANES:] = (gate * both[:, LANES:]).astype(BF16)
        return carry

    lax.fori_loop(0, seq, gated_body, 0)

    def second_body(m, carry):
        real, imag = forward(m, sig)
        f0r, f0i = spectra_of(m, 0)
        f1r, f1i = spectra_of(m, 1)
        gr, gi, br, bi = real[:, :LANES], imag[:, :LANES], real[:, LANES:], imag[:, LANES:]
        put(m, 0, *complex_product(gr, gi, f1r, f1i))
        put(m, 1, *conj_product(f0r, f0i, br, bi))
        return carry

    lax.fori_loop(0, 2 * length // TILE, second_body, 0)
    inverse(conv2, False)

    def last_body(c, carry):
        both = conv2[chunk(c), :]
        second, grad_value = both[:, :LANES], both[:, LANES:]
        staged[0, chunk(c), :] = (gates[1, chunk(c), :] * second).astype(BF16)
        cot[2, offset(c, 0), :] = (og[chunk(c), :].astype(F32) * second).astype(BF16).astype(F32)
        cot[0, offset(c, 0), :] = grad_value.astype(BF16).astype(F32)
        return carry

    lax.fori_loop(0, seq, last_body, 0)
    out_layer = exchange(LAYER, lambda d: staged.at[0, rows(d)], layer_out.at[:, lanes(me)])
    close(2)
    close(0)
    grads_of(2, 3)
    out_two = exchange(SG_TWO, lambda d: staged.at[3, rows(d)], stream_grads.at[2, :, lanes(me)])
    grads_of(0, 1)
    out_value = exchange(SG_VALUE, lambda d: staged.at[1, rows(d)], stream_grads.at[0, :, lanes(me)])
    for s in range(3):
        taps_of(s)
    out_taps = exchange(TAPS_OUT, lambda d: tap_send, tap_out.at[:, :, lanes(me)])
    outs = [out_one, out_layer, out_two, out_value, out_taps]
    for exchanged in outs:
        arrive(exchanged)
    for own, copies in sent + outs:
        for copy in copies:
            copy.wait_send()


def moved(streams, short_taps, long_filters, out_grad):
    seq = lax.axis_size("seq")
    streams_count, part_rows, blocks, channels = streams.shape
    part = part_rows * blocks
    length = part * seq
    fwd, inv = dft_tables(blocks, part_rows * seq)
    any_spec = pl.BlockSpec(memory_space=pl.ANY)
    hbm = pl.BlockSpec(memory_space=pltpu.HBM)
    vmem = pl.BlockSpec(memory_space=pltpu.VMEM)
    slots = 11
    layer, grads, taps = pl.pallas_call(
        functools.partial(kernel, seq, blocks),
        out_shape=(
            jax.ShapeDtypeStruct((part, channels), BF16),
            jax.ShapeDtypeStruct((3, part, channels), BF16),
            jax.ShapeDtypeStruct((3, 3, channels), F32),
        ),
        in_specs=[hbm, vmem, hbm, hbm, hbm, hbm],
        out_specs=(any_spec, any_spec, any_spec),
        scratch_shapes=[
            pltpu.VMEM((2, 2 * length, length), BF16),
            pltpu.VMEM((2, length, 2 * length), BF16),
            pltpu.VMEM((length, 2 * LANES), BF16),
            pltpu.VMEM((3, length, LANES), BF16),
            pltpu.VMEM((length, LANES), BF16),
            pltpu.VMEM((3, length + 2 * blocks, LANES), F32),
            pltpu.VMEM((3, length + 2 * blocks, LANES), F32),
            pltpu.VMEM((2, length, LANES), F32),
            pltpu.VMEM((length, 2 * LANES), BF16),
            pltpu.VMEM((length, LANES), BF16),
            pltpu.VMEM((2 * length, 2 * LANES), F32),
            pltpu.VMEM((2 * length, 2 * LANES), BF16),
            pltpu.VMEM((length, 2 * LANES), F32),
            pltpu.VMEM((length, 2 * LANES), F32),
            pltpu.VMEM((4, length, LANES), BF16),
            pltpu.VMEM((3, 3, LANES), F32),
            pltpu.SemaphoreType.DMA((slots, seq)),
            pltpu.SemaphoreType.DMA((slots, seq)),
            pltpu.SemaphoreType.DMA((2,)),
        ],
        compiler_params=pltpu.CompilerParams(
            collective_id=0, has_side_effects=True, vmem_limit_bytes=48 * 1024 * 1024
        ),
    )(
        pltpu.with_memory_space_constraint(streams.reshape(3, part, channels), pltpu.HBM),
        short_taps,
        pltpu.with_memory_space_constraint(long_filters.reshape(2, part, channels), pltpu.HBM),
        pltpu.with_memory_space_constraint(out_grad.reshape(part, channels), pltpu.HBM),
        jnp.asarray(fwd),
        jnp.asarray(inv),
    )
    return (
        layer.reshape(part_rows, blocks, channels),
        grads.reshape(3, part_rows, blocks, channels),
        taps,
    )


def either(streams, short_taps, long_filters, out_grad):
    seq = lax.axis_size("seq")
    part_rows, blocks, channels = streams.shape[1:]
    length = part_rows * blocks * seq
    fits = (
        channels == LANES * seq
        and lax.axis_size("group") == 2
        and blocks == 8
        and part_rows * blocks % LANES == 0
        and length % TILE == 0
        and length <= 1024
    )
    return (moved if fits else local)(streams, short_taps, long_filters, out_grad)


def solution(mesh):
    in_specs = (
        P(None, "seq", "group", "tensor"),
        P(None, None, "tensor"),
        P(None, "seq", None, "tensor"),
        P("seq", "group", "tensor"),
    )
    out_specs = (
        P("seq", "group", "tensor"),
        P(None, "seq", "group", "tensor"),
        P("group", None, "tensor"),
    )
    return jax.shard_map(either, mesh=mesh, in_specs=in_specs, out_specs=out_specs, check_vma=False)
```

```python
import functools
import math

import jax
import jax.numpy as jnp
import ml_dtypes
import numpy as np
from jax import lax
from jax.experimental import pallas as pl
from jax.experimental.pallas import tpu as pltpu
from jax.sharding import PartitionSpec as P

HIGHEST_PRECISION = lax.Precision.HIGHEST
MESH = pl.DeviceIdType.MESH
LANES = 128
TILE = 256
F32 = jnp.float32
BF16 = jnp.bfloat16


def shifted(value, axis, by):
    count = lax.axis_size(axis)
    return lax.ppermute(value, axis, [(i, (i + by) % count) for i in range(count)])


def complex_product(left_real, left_imag, right_real, right_imag):
    return (
        left_real * right_real - left_imag * right_imag,
        left_real * right_imag + left_imag * right_real,
    )


def conj_product(left_real, left_imag, right_real, right_imag):
    return (
        left_real * right_real + left_imag * right_imag,
        left_real * right_imag - left_imag * right_real,
    )


def local(streams, short_taps, long_filters, out_grad):
    seq_count = lax.axis_size("seq")
    seq_place = lax.axis_index("seq")
    local_rows = streams.shape[1]
    channels = streams.shape[3]
    block_rows = local_rows * seq_count
    full_length = 2 * block_rows * seq_count
    angle_unit = math.pi / full_length
    block_pos = jnp.arange(seq_count, dtype=jnp.int32)
    odd_slots = 2 * block_pos + 1
    local_index = seq_place * local_rows + jnp.arange(local_rows, dtype=jnp.int32)
    row_pos = jnp.arange(block_rows, dtype=jnp.int32)
    start_pos = block_pos[None, :, None] * block_rows + local_index[:, None, None]
    fwd_angle = (start_pos * odd_slots[None, None, :] % (2 * full_length)).astype(
        jnp.float32
    ) * angle_unit
    fwd_table = jnp.stack([jnp.cos(fwd_angle), -jnp.sin(fwd_angle)], axis=-1)
    inner_angle = (row_pos[:, None] * row_pos[None, :] % block_rows).astype(jnp.float32) * (
        2.0 * math.pi / block_rows
    )
    inner_cos = jnp.cos(inner_angle)
    inner_sin = jnp.sin(inner_angle)
    inner_table = jnp.stack(
        [jnp.stack([inner_cos, -inner_sin], axis=-1), jnp.stack([inner_sin, inner_cos], axis=-1)],
        axis=0,
    )
    back_num = (
        row_pos[None, :]
        * (4 * seq_count * row_pos[:, None] + 2 * seq_place + 1)
        % (2 * full_length)
    )
    back_angle = back_num.astype(jnp.float32) * angle_unit
    back_cos = jnp.cos(back_angle)
    back_sin = jnp.sin(back_angle)
    back_table = jnp.stack(
        [jnp.stack([back_cos, back_sin], axis=-1), jnp.stack([-back_sin, back_cos], axis=-1)],
        axis=0,
    )
    outer_angle = (block_pos[:, None] * odd_slots[None, :] % (4 * seq_count)).astype(
        jnp.float32
    ) * (math.pi / (2 * seq_count))
    outer_table = jnp.stack([jnp.cos(outer_angle).T, -jnp.sin(outer_angle).T], axis=0)

    def previous_rows(block):
        edge = shifted(block[:, -1:], "seq", 1)
        rolled = jnp.concatenate([jnp.zeros_like(edge[:, :, :1]), edge[:, :, :-1]], axis=2)
        edge = jnp.where(seq_place == 0, rolled, edge)
        return jnp.concatenate([edge, block[:, :-1]], axis=1)

    def next_rows(block):
        edge = shifted(block[:, :1], "seq", -1)
        rolled = jnp.concatenate([edge[:, :, 1:], jnp.zeros_like(edge[:, :, :1])], axis=2)
        edge = jnp.where(seq_place == seq_count - 1, rolled, edge)
        return jnp.concatenate([block[:, 1:], edge], axis=1)

    def spectra(signals):
        count = signals.shape[0]
        twisted = jnp.einsum("simc,imjr->srijc", signals, fwd_table, precision=HIGHEST_PRECISION)
        slotted = lax.all_to_all(twisted, "seq", split_axis=3, concat_axis=2, tiled=True)
        slotted = slotted.reshape(count, 2, block_rows, channels)
        spec = jnp.einsum("sric,rikq->sqkc", slotted, inner_table, precision=HIGHEST_PRECISION)
        return (spec[:, 0], spec[:, 1])

    def signals_back(real_spec, imag_spec):
        count = real_spec.shape[0]
        stacked = jnp.stack([real_spec, imag_spec], axis=1)
        turned = jnp.einsum("srkc,rkiq->sqic", stacked, back_table, precision=HIGHEST_PRECISION)
        turned = turned.reshape(count, 2, block_rows, 1, channels)
        parts = lax.all_to_all(turned, "seq", split_axis=2, concat_axis=3, tiled=True)
        rows_out = jnp.einsum("srijc,rjm->simc", parts, outer_table, precision=HIGHEST_PRECISION)
        return rows_out * (2.0 / full_length)

    def tap_weight(index):
        return short_taps[:, index][:, None, None, :]

    prev_one = previous_rows(streams)
    prev_two = previous_rows(prev_one)
    filtered = (
        tap_weight(0) * streams + tap_weight(1) * prev_one + tap_weight(2) * prev_two
    ).astype(jnp.bfloat16)
    value_stream = filtered[0].astype(jnp.float32)
    gate_one = filtered[1].astype(jnp.float32)
    gate_two = filtered[2].astype(jnp.float32)
    filters = long_filters.astype(jnp.float32)
    real_first, imag_first = spectra(jnp.stack([value_stream, filters[0]]))
    product_one = complex_product(real_first[0], imag_first[0], real_first[1], imag_first[1])
    first_conv = signals_back(product_one[0][None], product_one[1][None])[0]
    gated_first = gate_one * first_conv
    real_second, imag_second = spectra(jnp.stack([gated_first, filters[1]]))
    product_two = complex_product(real_second[0], imag_second[0], real_second[1], imag_second[1])
    second_conv = signals_back(product_two[0][None], product_two[1][None])[0]
    layer_out = (gate_two * second_conv).astype(jnp.bfloat16)
    cotangent = out_grad.astype(jnp.float32)
    back_two = cotangent * gate_two
    grad_two = cotangent * second_conv
    real_third, imag_third = spectra(back_two[None])
    filter_two_real, filter_two_imag = (real_second[1], imag_second[1])
    correlated_two = conj_product(filter_two_real, filter_two_imag, real_third[0], imag_third[0])
    grad_gated = signals_back(correlated_two[0][None], correlated_two[1][None])[0]
    grad_one = grad_gated * first_conv
    back_one = grad_gated * gate_one
    real_fourth, imag_fourth = spectra(back_one[None])
    filter_one_real, filter_one_imag = (real_first[1], imag_first[1])
    correlated_one = conj_product(filter_one_real, filter_one_imag, real_fourth[0], imag_fourth[0])
    grad_value = signals_back(correlated_one[0][None], correlated_one[1][None])[0]
    stream_cot = jnp.stack([grad_value, grad_one, grad_two]).astype(jnp.bfloat16)
    next_one = next_rows(stream_cot)
    next_two = next_rows(next_one)
    stream_grads = (
        tap_weight(0) * stream_cot + tap_weight(1) * next_one + tap_weight(2) * next_two
    ).astype(jnp.bfloat16)
    cot_float = stream_cot.astype(jnp.float32)
    tap_terms = jnp.stack(
        [
            jnp.sum(cot_float * streams, axis=(1, 2)),
            jnp.sum(cot_float * prev_one, axis=(1, 2)),
            jnp.sum(cot_float * prev_two, axis=(1, 2)),
        ],
        axis=1,
    )
    tap_total = lax.psum(tap_terms, "seq")
    return (layer_out, stream_grads, tap_total * (1.0 / math.sqrt(block_rows * seq_count)))


def split_table(table):
    high = table.astype(ml_dtypes.bfloat16)
    low = (table - high.astype(np.float64)).astype(ml_dtypes.bfloat16)
    return np.stack([high, low])


def dft_tables(blocks, rows):
    length = blocks * rows
    place = np.arange(length)
    time = (place % blocks) * rows + place // blocks
    half = TILE // 2
    freq = np.arange(length).reshape(-1, half)
    angle = ((2 * freq[:, :, None] + 1) * time[None, None, :] % (4 * length)) * (math.pi / (2 * length))
    table = np.concatenate([np.cos(angle), -np.sin(angle)], axis=1).reshape(2 * length, length)
    return split_table(table), split_table(table.T / length)


FILTER0, FILTER1, VALUE, GATE_TWO, OUT_GRAD, GATE_ONE, SG_ONE, LAYER, SG_TWO, SG_VALUE, TAPS_OUT = range(11)


def kernel(
    seq, blocks, streams, taps, filters, out_grad, fwd_hbm, inv_hbm,
    layer_out, stream_grads, tap_out,
    fwd, inv, xf, sb, og, s32, cot, gates, sig, sig_low, spec_f, prod, conv, conv2, staged, tap_send,
    send_sem, recv_sem, table_sem,
):
    me = lax.axis_index("seq")
    group = lax.axis_index("group")
    other = 1 - group
    part = streams.shape[1]
    length = part * seq
    half = TILE // 2
    order = sorted(range(1, seq), key=lambda k: abs(k - seq / 2))

    def peer(k):
        return lax.rem(me + k, seq)

    def lanes(d):
        return pl.ds(pl.multiple_of(d * LANES, LANES), LANES)

    def rows(d):
        return pl.ds(pl.multiple_of(d * part, part), part)

    def remote(slot, k, src, dst):
        return pltpu.make_async_remote_copy(
            src_ref=src, dst_ref=dst, send_sem=send_sem.at[slot, k], recv_sem=recv_sem.at[slot, k],
            device_id={"seq": peer(k)}, device_id_type=MESH,
        )

    def exchange(slot, src_of, dst):
        own = pltpu.make_async_copy(src_of(me), dst, recv_sem.at[slot, 0])
        copies = [remote(slot, k, src_of(peer(k)), dst) for k in order]
        for copy in copies:
            copy.start()
        own.start()
        return own, copies

    def arrive(exchanged):
        own, copies = exchanged
        own.wait()
        for copy in copies:
            copy.wait_recv()

    barrier = pltpu.get_barrier_semaphore()
    for k in range(1, seq):
        pl.semaphore_signal(barrier, inc=1, device_id={"seq": peer(k)}, device_id_type=MESH)
    pl.semaphore_signal(barrier, inc=1, device_id={"group": other}, device_id_type=MESH)
    fwd_copy = pltpu.make_async_copy(fwd_hbm, fwd, table_sem.at[0])
    inv_copy = pltpu.make_async_copy(inv_hbm, inv, table_sem.at[1])
    pl.semaphore_wait(barrier, seq)

    mine = rows(me)
    in_f = exchange(FILTER0, lambda d: filters.at[group, :, lanes(d)], xf.at[mine, lanes(group)])
    own_f1 = pltpu.make_async_copy(
        filters.at[other, :, lanes(me)], xf.at[mine, lanes(other)], recv_sem.at[FILTER1, 0]
    )
    own_f1.start()
    fwd_copy.start()
    in_v = exchange(VALUE, lambda d: streams.at[0, :, lanes(d)], sb.at[0, mine])
    in_g2 = exchange(GATE_TWO, lambda d: streams.at[2, :, lanes(d)], sb.at[2, mine])
    in_og = exchange(OUT_GRAD, lambda d: out_grad.at[:, lanes(d)], og.at[mine])
    in_g1 = exchange(GATE_ONE, lambda d: streams.at[1, :, lanes(d)], sb.at[1, mine])
    inv_copy.start()
    sent = [in_f, in_v, in_g2, in_og, in_g1]

    pad = 2 * blocks
    sub = lax.broadcasted_iota(jnp.int32, (blocks, LANES), 0)

    def tap(s, j):
        return taps[s, pl.ds(j, 1), lanes(me)]

    def chunk(c):
        return pl.ds(pl.multiple_of(c * part, part), part)

    def offset(c, by):
        return pl.ds(pl.multiple_of(c * part + by, blocks), part)

    def widen(s):
        def body(c, carry):
            s32[s, offset(c, pad), :] = sb[s, chunk(c), :].astype(F32)
            return carry

        lax.fori_loop(0, seq, body, 0, unroll=4)
        for step in range(2):
            edge = s32[s, pl.ds(length + step * blocks, blocks), :]
            s32[s, pl.ds(step * blocks, blocks), :] = jnp.where(sub == 0, 0.0, pltpu.roll(edge, 1, 0))

    def filtered(s, c):
        total = tap(s, 0) * s32[s, offset(c, pad), :]
        total = total + tap(s, 1) * s32[s, offset(c, blocks), :]
        total = total + tap(s, 2) * s32[s, offset(c, 0), :]
        return total.astype(BF16)

    def cots(s, c):
        base = [cot[s, offset(c, j * blocks), :] for j in range(3)]
        total = tap(s, 0) * base[0] + tap(s, 1) * base[1] + tap(s, 2) * base[2]
        return total.astype(BF16)

    def close(s):
        for step in range(2):
            edge = cot[s, pl.ds(step * blocks, blocks), :]
            cot[s, pl.ds(length + step * blocks, blocks), :] = jnp.where(
                sub == blocks - 1, 0.0, pltpu.roll(edge, blocks - 1, 0)
            )

    def grads_of(s, slot):
        def body(c, carry):
            staged[slot, chunk(c), :] = cots(s, c)
            return carry

        lax.fori_loop(0, seq, body, 0, unroll=4)

    def taps_of(s):
        def body(c, sums):
            now = cot[s, offset(c, 0), :]
            return tuple(
                sums[j]
                + jnp.sum(
                    (now * s32[s, offset(c, pad - j * blocks), :]).reshape(-1, 8, LANES), axis=0
                )
                for j in range(3)
            )

        sums = lax.fori_loop(0, seq, body, tuple(jnp.zeros((8, LANES), F32) for _ in range(3)), unroll=4)
        for j in range(3):
            tap_send[s, pl.ds(j, 1), :] = jnp.sum(sums[j], axis=0, keepdims=True) * (
                1.0 / math.sqrt(length)
            )

    def tile(m):
        return pl.ds(pl.multiple_of(m * TILE, TILE), TILE)

    def forward(m, signals):
        out = jnp.dot(fwd[0, tile(m), :], signals[...], preferred_element_type=F32)
        return out[:half], out[half:]

    def put(m, col, real, imag):
        prod[pl.ds(pl.multiple_of(m * TILE, TILE), half), col * LANES:(col + 1) * LANES] = real.astype(BF16)
        prod[pl.ds(pl.multiple_of(m * TILE + half, half), half), col * LANES:(col + 1) * LANES] = imag.astype(BF16)

    def spectra_of(m, col):
        cols = slice(col * LANES, (col + 1) * LANES)
        return (
            spec_f[pl.ds(pl.multiple_of(m * TILE, TILE), half), cols],
            spec_f[pl.ds(pl.multiple_of(m * TILE + half, half), half), cols],
        )

    def inverse(into, split):
        def body(m, carry):
            out = jnp.dot(inv[0, tile(m), :], prod[...], preferred_element_type=F32)
            if split:
                out = out + jnp.dot(inv[1, tile(m), :], prod[...], preferred_element_type=F32)
            into[tile(m), :] = out
            return carry

        lax.fori_loop(0, length // TILE, body, 0, unroll=4)

    in_f[0].wait()
    handed = []
    for k, copy in zip(order, in_f[1]):
        copy.wait_recv()
        piece = xf.at[rows(lax.rem(me - k + seq, seq)), lanes(group)]
        hand = pltpu.make_async_remote_copy(
            src_ref=piece, dst_ref=piece, send_sem=send_sem.at[FILTER1, k],
            recv_sem=recv_sem.at[FILTER1, k], device_id={"group": other}, device_id_type=MESH,
        )
        hand.start()
        handed.append(hand)
    sent.append((own_f1, handed))
    arrive((own_f1, handed))
    fwd_copy.wait()

    def filter_body(m, carry):
        out = jnp.dot(fwd[0, tile(m), :], xf[...], preferred_element_type=F32)
        spec_f[tile(m), :] = out + jnp.dot(fwd[1, tile(m), :], xf[...], preferred_element_type=F32)
        return carry

    lax.fori_loop(0, 2 * length // TILE, filter_body, 0, unroll=4)

    arrive(in_v)
    widen(0)

    def value_body(c, carry):
        sig[chunk(c), 0:LANES] = filtered(0, c)
        return carry

    lax.fori_loop(0, seq, value_body, 0, unroll=4)
    arrive(in_g2)
    widen(2)

    arrive(in_og)

    def back_body(c, carry):
        gate = filtered(2, c)
        gates[1, chunk(c), :] = gate.astype(F32)
        back = og[chunk(c), :].astype(F32) * gate.astype(F32)
        sig[chunk(c), LANES:] = back.astype(BF16)
        sig_low[chunk(c), :] = (back - back.astype(BF16).astype(F32)).astype(BF16)
        return carry

    lax.fori_loop(0, seq, back_body, 0, unroll=4)

    def first_body(m, carry):
        out = jnp.dot(fwd[0, tile(m), :], sig[...], preferred_element_type=F32)
        out = out + jnp.dot(fwd[1, tile(m), :], sig[...], preferred_element_type=F32)
        low = jnp.dot(fwd[0, tile(m), :], sig_low[...], preferred_element_type=F32)
        back = out[:, LANES:] + low
        f0r, f0i = spectra_of(m, 0)
        f1r, f1i = spectra_of(m, 1)
        first = complex_product(out[:half, :LANES], out[half:, :LANES], f0r, f0i)
        second = conj_product(f1r, f1i, back[:half], back[half:])
        put(m, 0, *first)
        put(m, 1, *second)
        return carry

    lax.fori_loop(0, 2 * length // TILE, first_body, 0, unroll=4)
    inv_copy.wait()
    inverse(conv, True)

    def one_body(c, carry):
        both = conv[chunk(c), :]
        cot[1, offset(c, 0), :] = (both[:, LANES:] * both[:, :LANES]).astype(BF16).astype(F32)
        return carry

    lax.fori_loop(0, seq, one_body, 0, unroll=4)
    close(1)
    grads_of(1, 2)
    out_one = exchange(SG_ONE, lambda d: staged.at[2, rows(d)], stream_grads.at[1, :, lanes(me)])
    arrive(in_g1)
    widen(1)

    def gated_body(c, carry):
        gate = filtered(1, c).astype(F32)
        both = conv[chunk(c), :]
        sig[chunk(c), 0:LANES] = (gate * both[:, :LANES]).astype(BF16)
        sig[chunk(c), LANES:] = (gate * both[:, LANES:]).astype(BF16)
        return carry

    lax.fori_loop(0, seq, gated_body, 0, unroll=4)

    def second_body(m, carry):
        real, imag = forward(m, sig)
        f0r, f0i = spectra_of(m, 0)
        f1r, f1i = spectra_of(m, 1)
        gr, gi, br, bi = real[:, :LANES], imag[:, :LANES], real[:, LANES:], imag[:, LANES:]
        put(m, 0, *complex_product(gr, gi, f1r, f1i))
        put(m, 1, *conj_product(f0r, f0i, br, bi))
        return carry

    lax.fori_loop(0, 2 * length // TILE, second_body, 0, unroll=4)
    inverse(conv2, False)

    def last_body(c, carry):
        both = conv2[chunk(c), :]
        second, grad_value = both[:, :LANES], both[:, LANES:]
        staged[0, chunk(c), :] = (gates[1, chunk(c), :] * second).astype(BF16)
        cot[2, offset(c, 0), :] = (og[chunk(c), :].astype(F32) * second).astype(BF16).astype(F32)
        cot[0, offset(c, 0), :] = grad_value.astype(BF16).astype(F32)
        return carry

    lax.fori_loop(0, seq, last_body, 0, unroll=4)
    out_layer = exchange(LAYER, lambda d: staged.at[0, rows(d)], layer_out.at[:, lanes(me)])
    close(2)
    close(0)
    grads_of(2, 3)
    out_two = exchange(SG_TWO, lambda d: staged.at[3, rows(d)], stream_grads.at[2, :, lanes(me)])
    grads_of(0, 1)
    out_value = exchange(SG_VALUE, lambda d: staged.at[1, rows(d)], stream_grads.at[0, :, lanes(me)])
    for s in range(3):
        taps_of(s)
    out_taps = exchange(TAPS_OUT, lambda d: tap_send, tap_out.at[:, :, lanes(me)])
    outs = [out_one, out_layer, out_two, out_value, out_taps]
    for exchanged in outs:
        arrive(exchanged)
    for own, copies in sent + outs:
        for copy in copies:
            copy.wait_send()


def moved(streams, short_taps, long_filters, out_grad):
    seq = lax.axis_size("seq")
    streams_count, part_rows, blocks, channels = streams.shape
    part = part_rows * blocks
    length = part * seq
    fwd, inv = dft_tables(blocks, part_rows * seq)
    any_spec = pl.BlockSpec(memory_space=pl.ANY)
    hbm = pl.BlockSpec(memory_space=pltpu.HBM)
    vmem = pl.BlockSpec(memory_space=pltpu.VMEM)
    slots = 11
    layer, grads, taps = pl.pallas_call(
        functools.partial(kernel, seq, blocks),
        out_shape=(
            jax.ShapeDtypeStruct((part, channels), BF16),
            jax.ShapeDtypeStruct((3, part, channels), BF16),
            jax.ShapeDtypeStruct((3, 3, channels), F32),
        ),
        in_specs=[hbm, vmem, hbm, hbm, hbm, hbm],
        out_specs=(any_spec, any_spec, any_spec),
        scratch_shapes=[
            pltpu.VMEM((2, 2 * length, length), BF16),
            pltpu.VMEM((2, length, 2 * length), BF16),
            pltpu.VMEM((length, 2 * LANES), BF16),
            pltpu.VMEM((3, length, LANES), BF16),
            pltpu.VMEM((length, LANES), BF16),
            pltpu.VMEM((3, length + 2 * blocks, LANES), F32),
            pltpu.VMEM((3, length + 2 * blocks, LANES), F32),
            pltpu.VMEM((2, length, LANES), F32),
            pltpu.VMEM((length, 2 * LANES), BF16),
            pltpu.VMEM((length, LANES), BF16),
            pltpu.VMEM((2 * length, 2 * LANES), F32),
            pltpu.VMEM((2 * length, 2 * LANES), BF16),
            pltpu.VMEM((length, 2 * LANES), F32),
            pltpu.VMEM((length, 2 * LANES), F32),
            pltpu.VMEM((4, length, LANES), BF16),
            pltpu.VMEM((3, 3, LANES), F32),
            pltpu.SemaphoreType.DMA((slots, seq)),
            pltpu.SemaphoreType.DMA((slots, seq)),
            pltpu.SemaphoreType.DMA((2,)),
        ],
        compiler_params=pltpu.CompilerParams(
            collective_id=0, has_side_effects=True, vmem_limit_bytes=48 * 1024 * 1024
        ),
    )(
        pltpu.with_memory_space_constraint(streams.reshape(3, part, channels), pltpu.HBM),
        short_taps,
        pltpu.with_memory_space_constraint(long_filters.reshape(2, part, channels), pltpu.HBM),
        pltpu.with_memory_space_constraint(out_grad.reshape(part, channels), pltpu.HBM),
        jnp.asarray(fwd),
        jnp.asarray(inv),
    )
    return (
        layer.reshape(part_rows, blocks, channels),
        grads.reshape(3, part_rows, blocks, channels),
        taps,
    )


def either(streams, short_taps, long_filters, out_grad):
    seq = lax.axis_size("seq")
    part_rows, blocks, channels = streams.shape[1:]
    length = part_rows * blocks * seq
    fits = (
        channels == LANES * seq
        and lax.axis_size("group") == 2
        and blocks == 8
        and part_rows * blocks % LANES == 0
        and length % TILE == 0
        and length <= 1024
    )
    return (moved if fits else local)(streams, short_taps, long_filters, out_grad)


def solution(mesh):
    in_specs = (
        P(None, "seq", "group", "tensor"),
        P(None, None, "tensor"),
        P(None, "seq", None, "tensor"),
        P("seq", "group", "tensor"),
    )
    out_specs = (
        P("seq", "group", "tensor"),
        P(None, "seq", "group", "tensor"),
        P("group", None, "tensor"),
    )
    return jax.shard_map(either, mesh=mesh, in_specs=in_specs, out_specs=out_specs, check_vma=False)
```
